32 devices in a mesh: ctx: 8 (over y, x, core), tp: 4 (over z).
Axes of the slice: x: 2, y: 2, z: 4, core: 2. Of those that a mesh axis runs over, the one named last changes fastest.
Arguments:
- residual: bfloat16 [2048, 4096], P('ctx', 'tp'), may hold values from -6 to 6
- proj: bfloat16 [2048, 3, 4096], P('ctx', None, 'tp'), may hold values from -5 to 5
- short_filter: bfloat16 [7, 3, 4096], P(None, None, 'tp'), may hold values from -2.5 to 2.5
- medium_filter: bfloat16 [128, 4096], P(None, 'tp'), may hold values from -4 to 4
- skip: float32 [4096], P('tp'), may hold values from -3 to 3
- out_weight: bfloat16 [4096, 4096], P('ctx', 'tp'), may hold values from -0.09375 to 0.09375
Outputs:
- block_out: bfloat16 [2048, 4096], P('ctx', 'tp')
The draws below stay inside these ranges and needn't reach their ends.
All inputs are finite; a program needn't handle non-finite values.
Results may differ from the reference program's by a relative error of at most 0.0085.
Values may be sent and summed in bfloat16 or wider, within the bound.
A program may use at most 64 MiB of HBM per device.

```python
import jax
import jax.numpy as jnp
from jax import lax

D = 4096
SHORT = 7
MEDIUM = 128
TOKENS = 2048


def draw_medium_filter(key, part):
    first, second = jax.random.split(jax.random.fold_in(key, 11))
    lower, upper = (0.25, 6.0)
    spans = jnp.exp(jax.random.uniform(first, (1, D), jnp.float32, jnp.log(lower), jnp.log(upper)))
    decay = spans / MEDIUM
    lags = jnp.arange(MEDIUM, dtype=jnp.float32)[:, None]
    scale = jnp.sqrt(2.0 * decay / (1.0 - jnp.exp(-2.0 * spans)))
    values = jax.random.truncated_normal(second, -3.0, 3.0, (MEDIUM, D), jnp.float32)
    return (values * jnp.exp(-decay * lags) * scale).astype(jnp.bfloat16)


def block_scale(stream_key, extent, shards, low, largest):
    loudness = 1.0
    for axis_at, parts in shards:
        heights = jax.random.uniform(jax.random.fold_in(jax.random.fold_in(stream_key, 6), axis_at), (parts,), jnp.float32, low / len(shards), largest / len(shards))
        loudness = loudness * jnp.repeat(jnp.exp(heights), extent[axis_at] // parts).reshape((-1,) + (1,) * (len(extent) - 1 - axis_at))
    return loudness


def bell_draw(own_key, extent, scale, limit, pieces=(), kind=jnp.bfloat16):
    result = scale * jax.random.normal(own_key, extent, jnp.float32)
    if pieces:
        result = result * block_scale(own_key, extent, pieces, -0.22, 0.18)
    return jnp.clip(result, -limit, limit).astype(kind)


def setup_inputs(seed: int = 0) -> dict:
    streams_of = jax.random.split(jax.random.key(seed), 7)
    residual = bell_draw(streams_of[0], (TOKENS, D), 1.0, 6.0, ((0, 8), (1, 4)))
    proj = bell_draw(streams_of[1], (TOKENS, 3, D), 1.0, 5.0, ((0, 8), (2, 4)))
    short_filter = bell_draw(streams_of[2], (SHORT, 3, D), 0.4, 2.5, ((2, 4),))
    medium_filter = draw_medium_filter(jax.random.fold_in(streams_of[6], 71), 0)
    skip = bell_draw(streams_of[4], (D,), 1.0, 3.0, ((0, 4),), jnp.float32)
    out_weight = bell_draw(streams_of[5], (D, D), D ** -0.5, 0.09375, ((0, 8), (1, 4)))
    return {"residual": residual, "proj": proj, "short_filter": short_filter, "medium_filter": medium_filter, "skip": skip, "out_weight": out_weight}


def channel_block(args):
    streams, short_f, medium_f, skip_b = args
    tokens = streams.shape[0]
    taps = short_f.shape[0]
    padded = jnp.concatenate([jnp.zeros((taps - 1,) + streams.shape[1:], jnp.float32), streams.astype(jnp.float32)], 0)
    mixed = jnp.zeros(streams.shape, jnp.float32)
    for j in range(taps):
        mixed = mixed + short_f[j].astype(jnp.float32) * padded[taps - 1 - j: taps - 1 - j + tokens]
    product = (mixed[:, 1] * mixed[:, 2]).astype(jnp.bfloat16)
    length = 2 * tokens
    spectrum = jnp.fft.rfft(product.astype(jnp.float32), n=length, axis=0) * jnp.fft.rfft(medium_f.astype(jnp.float32), n=length, axis=0)
    filtered = jnp.fft.irfft(spectrum, n=length, axis=0)[:tokens]
    filtered = filtered + skip_b * product.astype(jnp.float32)
    return (mixed[:, 0] * filtered).astype(jnp.bfloat16)


def reference(residual, proj, short_filter, medium_filter, skip, out_weight):
    width = 256
    groups = D // width
    streams = jnp.moveaxis(proj.reshape(TOKENS, 3, groups, width), 2, 0)
    short_g = jnp.moveaxis(short_filter.reshape(SHORT, 3, groups, width), 2, 0)
    medium_g = jnp.moveaxis(medium_filter.reshape(MEDIUM, groups, width), 1, 0)
    skip_g = skip.reshape(groups, width)
    gated = lax.map(channel_block, (streams, short_g, medium_g, skip_g))
    gated = jnp.moveaxis(gated, 0, 1).reshape(TOKENS, D)
    total = jnp.dot(gated, out_weight, preferred_element_type=jnp.float32)
    return (residual.astype(jnp.float32) + total).astype(jnp.bfloat16)
```

```python
import functools

import jax
import jax.numpy as jnp
import numpy as np
from jax import lax
from jax.experimental import pallas as pl
from jax.experimental.pallas import tpu as pltpu
from jax.sharding import PartitionSpec as P

WIDE = 256
STEP = 128
EDGE = 16
MESH = pl.DeviceIdType.MESH


def spectrum_tables(length, reach):
    half = length // 2
    angle = 2 * np.pi / length * np.outer(np.arange(half) + 0.5, np.arange(length))
    forward = np.concatenate([np.cos(angle), np.sin(angle)], 0)
    inverse = (2.0 / length) * forward.T[reach:]

    def two(table):
        high = table.astype(np.float32).astype(jnp.bfloat16)
        return high, (table - high.astype(np.float64)).astype(np.float32).astype(jnp.bfloat16)

    return two(forward) + two(inverse)


def dot(a, b):
    return jnp.dot(a, b, preferred_element_type=jnp.float32)


def kernel(
    n_ctx, n_tp, taps,
    residual, proj, short, medium, skip, weight, fwd_hi, fwd_lo, inv_hi, inv_lo,
    out,
    whole, gated, total, wide, short32, product, transfer, query, spec, spec_hi, spec_lo, edge,
    own_sem, w_send, w_recv, z_send, z_recv, edge_send, edge_recv, tail_send, tail_recv,
):
    rows, chans = residual.shape[0], proj.shape[2]
    depth, outs = weight.shape
    reach = medium.shape[0]
    chunks = chans // WIDE
    length = rows + reach
    half = length // 2
    me, z = lax.axis_index("ctx"), lax.axis_index("tp")
    after, before = lax.rem(me + 1, n_ctx), lax.rem(me + n_ctx - 1, n_ctx)
    square = n_ctx == 8 and n_tp == 4 and chans == 2 * depth

    def flip(bit):
        return me + bit - 2 * bit * lax.rem(me // bit, 2)

    if square:
        core, side, up = flip(1), flip(2), flip(4)
        corner = side + up - me

    barrier = pltpu.get_barrier_semaphore()

    def greet(where):
        pl.semaphore_signal(barrier, inc=1, device_id=where, device_id_type=MESH)

    if square:
        for peer in (core, side, up, after, before):
            greet({"ctx": peer})
        greeted = 5
    else:
        @pl.loop(1, n_ctx)
        def _(by):
            greet({"ctx": lax.rem(me + by, n_ctx)})
        greeted = n_ctx - 1

    @pl.when(z < n_tp - 1)
    def _():
        greet({"tp": z + 1})

    @pl.when(z > 0)
    def _():
        greet({"tp": z - 1})

    def columns(q):
        return pl.ds(pl.multiple_of(q * WIDE, WIDE), WIDE)

    def edge_copy():
        return pltpu.make_async_remote_copy(
            src_ref=proj.at[:, pl.ds(rows - EDGE, EDGE), :], dst_ref=edge,
            send_sem=edge_send, recv_sem=edge_recv, device_id={"ctx": after}, device_id_type=MESH)

    def tail_copy(q):
        return pltpu.make_async_remote_copy(
            src_ref=product.at[pl.ds(rows, reach), columns(q)],
            dst_ref=product.at[pl.ds(0, reach), columns(q)],
            send_sem=tail_send.at[q], recv_sem=tail_recv.at[q],
            device_id={"ctx": after}, device_id_type=MESH)

    def z_copy(way, step, q, origin):
        return pltpu.make_async_remote_copy(
            src_ref=gated.at[origin, q], dst_ref=gated.at[origin, q],
            send_sem=z_send.at[way, step, q], recv_sem=z_recv.at[way, step, q],
            device_id={"tp": z + 1 if way == 0 else z - 1}, device_id_type=MESH)

    def z_sends(step, q, act):
        @pl.when((z < n_tp - 1) & (z >= step))
        def _():
            act(z_copy(0, step, q, z - step))

        @pl.when((z > 0) & (z + step <= n_tp - 1))
        def _():
            act(z_copy(1, step, q, z + step))

    def z_wait(step, q):
        @pl.when(z - 1 - step >= 0)
        def _():
            z_copy(0, step, q, z - 1 - step).wait_recv()

        @pl.when(z + 1 + step <= n_tp - 1)
        def _():
            z_copy(1, step, q, z + 1 + step).wait_recv()

    def z_pass(step, q):
        z_wait(step, q)
        if step + 1 < n_tp - 1:
            z_sends(step + 1, q, lambda copy: copy.start())

    part = depth // 2

    def w_rows(block, h):
        return pl.ds(pl.multiple_of(block * depth + h * part, part), part)

    def w_copy(slot, block, h, to, own=False):
        return pltpu.make_async_remote_copy(
            src_ref=weight.at[pl.ds(h * part, part), :] if own else whole.at[w_rows(block, h), :],
            dst_ref=whole.at[w_rows(block, h), :],
            send_sem=w_send.at[slot], recv_sem=w_recv.at[slot],
            device_id={"ctx": to}, device_id_type=MESH)

    def w_all(by):
        return pltpu.make_async_remote_copy(
            src_ref=weight, dst_ref=whole.at[pl.ds(pl.multiple_of(me * depth, depth), depth), :],
            send_sem=w_send.at[by], recv_sem=w_recv.at[by],
            device_id={"ctx": lax.rem(me + by, n_ctx)}, device_id_type=MESH)

    own = pltpu.make_async_copy(
        weight, whole.at[pl.ds(pl.multiple_of(me * depth, depth), depth), :], own_sem)

    def mixed(stream, start, cols):
        acc = None
        for j in range(taps):
            term = short32[stream, j : j + 1, cols] * wide[stream, pl.ds(EDGE + start - j, STEP), cols]
            acc = term if acc is None else acc + term
        return acc

    def multiply(start, cols):
        product[pl.ds(reach + start, STEP), cols] = (
            mixed(1, start, cols) * mixed(2, start, cols)
        ).astype(jnp.bfloat16)

    for stream in range(3):
        short32[stream, 0:taps, :] = short[stream].astype(jnp.float32)

    @pl.loop(0, chunks)
    def _(q):
        cols = columns(q)
        for stream in range(3):
            wide[stream, pl.ds(EDGE, rows), cols] = proj[stream, :, cols].astype(jnp.float32)

    pl.semaphore_wait(barrier, greeted + jnp.where(z < n_tp - 1, 1, 0) + jnp.where(z > 0, 1, 0))
    edge_copy().start()

    @pl.loop(0, chunks)
    def _(q):
        for start in range(rows - reach, rows, STEP):
            multiply(start, columns(q))
        tail_copy(q).start()

    own.start()
    sent = []
    if square:
        for slot, h, to in ((0, 0, side), (1, 1, up), (2, 1, side), (3, 0, up), (4, 0, core), (5, 1, core)):
            sent.append(w_copy(slot, me, h, to, own=True))
            sent[-1].start()
    else:
        @pl.loop(1, n_ctx)
        def _(by):
            w_all(by).start()

    @pl.loop(0, chunks)
    def _(q):
        taps_now = medium[:, columns(q)]
        transfer[:, columns(q)] = dot(fwd_hi[:, 0:reach], taps_now) + dot(fwd_lo[:, 0:reach], taps_now)

    edge_copy().wait_recv()
    for stream in range(3):
        wide[stream, 0:EDGE, :] = jnp.where(me > 0, edge[stream].astype(jnp.float32), 0.0)

    @pl.loop(0, chunks)
    def _(q):
        cols = columns(q)
        for start in range(0, rows - reach, STEP):
            multiply(start, cols)
        for start in range(0, rows, STEP):
            query[pl.ds(start, STEP), :] = mixed(0, start, cols)
        tail_copy(q).wait_recv()

        @pl.when(me == 0)
        def _():
            product[0:reach, cols] = jnp.zeros((reach, WIDE), jnp.bfloat16)

        window = product[:, cols]
        spec[...] = dot(fwd_hi[...], window) + dot(fwd_lo[...], window)
        for top in range(0, half, 64):
            a, b = spec[top : top + 64, :], spec[half + top : half + top + 64, :]
            c, d = transfer[top : top + 64, cols], transfer[half + top : half + top + 64, cols]
            for at, value in ((top, a * c - b * d), (half + top, a * d + b * c)):
                high = value.astype(jnp.bfloat16)
                spec_hi[at : at + 64, :] = high
                spec_lo[at : at + 64, :] = (value - high.astype(jnp.float32)).astype(jnp.bfloat16)
        filtered = dot(inv_hi[...], spec_hi[...]) + dot(inv_hi[...], spec_lo[...]) + dot(inv_lo[...], spec_hi[...])
        filtered = filtered + skip[:, cols] * product[pl.ds(reach, rows), cols].astype(jnp.float32)
        gated[z, q] = (query[...] * filtered).astype(jnp.bfloat16)
        z_sends(0, q, lambda copy: copy.start())

        @pl.when(q >= 1)
        def _():
            z_pass(0, q - 1)

    def project(origin, first, count):
        @pl.loop(0, outs // WIDE)
        def _(tile):
            cols = columns(tile)
            acc = total[:, cols]
            for q in range(first, first + count):
                at = pl.multiple_of(origin * chans + q * WIDE, WIDE)
                acc = acc + dot(gated[origin, q], whole[pl.ds(at, WIDE), cols])
            total[:, cols] = acc

    total[...] = residual[...].astype(jnp.float32)

    def near(origin):
        return (origin - z <= n_tp - 2) & (z - origin <= n_tp - 2)

    if square:
        far = corner // 2

        def arrived(slot, block, h):
            w_copy(slot, block, h, core).wait_recv()

        def relay(slot, block, h, to):
            copy = w_copy(slot, block, h, to)
            copy.start()
            sent.append(copy)

        arrived(0, side, 0)
        relay(6, side, 0, up)
        relay(8, side, 0, core)
        arrived(1, up, 1)
        relay(7, up, 1, side)
        relay(9, up, 1, core)
        z_pass(0, chunks - 1)
        for q in range(chunks - 1):
            z_pass(1, q)
        arrived(2, side, 1)
        relay(10, side, 1, core)
        arrived(3, up, 0)
        relay(11, up, 0, core)
        z_pass(1, chunks - 1)
        own.wait()
        for slot, block, h in ((4, core, 0), (5, core, 1)):
            arrived(slot, block, h)
        other = core - me
        for slot, block, h in ((8, side, 0), (9, up, 1), (10, side, 1), (11, up, 0)):
            arrived(slot, block + other, h)

        @pl.loop(0, n_tp)
        def _(origin):
            @pl.when(near(origin) & (origin != far))
            def _():
                project(origin, 0, chunks)

        arrived(6, corner, 0)
        relay(12, corner, 0, core)
        arrived(7, corner, 1)
        relay(13, corner, 1, core)
        arrived(12, corner + other, 0)
        arrived(13, corner + other, 1)

        @pl.when(near(far))
        def _():
            project(far, 0, chunks)
    else:
        z_pass(0, chunks - 1)
        for step in range(1, n_tp - 2):
            @pl.loop(0, chunks)
            def _(q):
                z_pass(step, q)
        own.wait()

        @pl.loop(1, n_ctx)
        def _(by):
            w_all(by).wait_recv()

        @pl.loop(0, n_tp)
        def _(origin):
            @pl.when(near(origin))
            def _():
                project(origin, 0, chunks)

    for q in range(chunks):
        z_wait(n_tp - 2, q)

        @pl.when((z == 0) | (z == n_tp - 1))
        def _():
            project(n_tp - 1 - z, q, 1)

    out[...] = total[...].astype(jnp.bfloat16)

    edge_copy().wait_send()
    for q in range(chunks):
        tail_copy(q).wait_send()
    if square:
        for copy in sent:
            copy.wait_send()
    else:
        @pl.loop(1, n_ctx)
        def _(by):
            w_all(by).wait_send()
    for step in range(n_tp - 1):
        @pl.loop(0, chunks)
        def _(q):
            z_sends(step, q, lambda copy: copy.wait_send())


def on_device(n_ctx, n_tp, residual, proj, short_filter, medium_filter, skip, out_weight):
    rows, _, chans = proj.shape
    depth, outs = out_weight.shape
    taps, reach = short_filter.shape[0], medium_filter.shape[0]
    length, chunks = rows + reach, chans // WIDE
    tables = [jnp.asarray(table) for table in spectrum_tables(length, reach)]
    in_vmem = pl.BlockSpec(memory_space=pltpu.VMEM)
    dma = pltpu.SemaphoreType.DMA
    return pl.pallas_call(
        functools.partial(kernel, n_ctx, n_tp, taps),
        out_shape=jax.ShapeDtypeStruct((rows, outs), jnp.bfloat16),
        in_specs=[in_vmem] * 5 + [pl.BlockSpec(memory_space=pl.ANY)] + [in_vmem] * 4,
        out_specs=in_vmem,
        scratch_shapes=[
            pltpu.VMEM((n_ctx * depth, outs), jnp.bfloat16),
            pltpu.VMEM((n_tp, chunks, rows, WIDE), jnp.bfloat16),
            pltpu.VMEM((rows, outs), jnp.float32),
            pltpu.VMEM((3, EDGE + rows, chans), jnp.float32),
            pltpu.VMEM((3, 8, chans), jnp.float32),
            pltpu.VMEM((length, chans), jnp.bfloat16),
            pltpu.VMEM((length, chans), jnp.float32),
            pltpu.VMEM((rows, WIDE), jnp.float32),
            pltpu.VMEM((length, WIDE), jnp.float32),
            pltpu.VMEM((length, WIDE), jnp.bfloat16),
            pltpu.VMEM((length, WIDE), jnp.bfloat16),
            pltpu.VMEM((3, EDGE, chans), jnp.bfloat16),
            dma,
            dma((max(n_ctx, 14),)),
            dma((max(n_ctx, 14),)),
            dma((2, n_tp - 1, chunks)),
            dma((2, n_tp - 1, chunks)),
            dma,
            dma,
            dma((chunks,)),
            dma((chunks,)),
        ],
        compiler_params=pltpu.CompilerParams(
            collective_id=0, has_side_effects=True, vmem_limit_bytes=48 * 2**20
        ),
        cost_estimate=pl.CostEstimate(
            flops=2 * rows * n_ctx * depth * outs, bytes_accessed=2 * rows * chans * 5, transcendentals=0
        ),
    )(
        residual, proj.transpose(1, 0, 2), short_filter.transpose(1, 0, 2), medium_filter,
        skip.reshape(1, chans), out_weight, *tables,
    )


def solution(mesh):
    in_specs = (
        P("ctx", "tp"),
        P("ctx", None, "tp"),
        P(None, None, "tp"),
        P(None, "tp"),
        P("tp"),
        P("ctx", "tp"),
    )
    return jax.shard_map(
        functools.partial(on_device, mesh.shape["ctx"], mesh.shape["tp"]),
        mesh=mesh, in_specs=in_specs, out_specs=P("ctx", "tp"), check_vma=False,
    )
```

```python
import functools

import jax
import jax.numpy as jnp
import numpy as np
from jax import lax
from jax.experimental import pallas as pl
from jax.experimental.pallas import tpu as pltpu
from jax.sharding import PartitionSpec as P

WIDE = 256
STEP = 128
EDGE = 16
MESH = pl.DeviceIdType.MESH


def spectrum_tables(length, reach):
    half = length // 2
    angle = 2 * np.pi / length * np.outer(np.arange(half) + 0.5, np.arange(length))
    forward = np.concatenate([np.cos(angle), np.sin(angle)], 0)
    inverse = (2.0 / length) * forward.T[reach:]

    return np.concatenate([forward, inverse], 0).astype(np.float32)


def dot(a, b):
    return jnp.dot(a, b, preferred_element_type=jnp.float32)


def kernel(
    n_ctx, n_tp, taps,
    residual_hbm, proj_hbm, short_hbm, medium_hbm, skip_hbm, weight,
    tables_hbm,
    out,
    residual, proj, short, medium, skip, tables32, tables,
    whole, gated, total, wide, short32, product, transfer, query, spec, spec_hi, spec_lo, edge,
    local_sem, own_sem, w_send, w_recv, z_send, z_recv, edge_send, edge_recv, tail_send, tail_recv,
):
    rows, chans = residual.shape[0], proj.shape[2]
    depth, outs = weight.shape
    reach = medium.shape[0]
    chunks = chans // WIDE
    length = rows + reach
    half = length // 2
    me, z = lax.axis_index("ctx"), lax.axis_index("tp")
    after, before = lax.rem(me + 1, n_ctx), lax.rem(me + n_ctx - 1, n_ctx)
    square = n_ctx == 8 and n_tp == 4 and chans == 2 * depth

    def flip(bit):
        return me + bit - 2 * bit * lax.rem(me // bit, 2)

    if square:
        core, side, up = flip(1), flip(2), flip(4)
        corner = side + up - me

    barrier = pltpu.get_barrier_semaphore()

    def greet(where):
        pl.semaphore_signal(barrier, inc=1, device_id=where, device_id_type=MESH)

    if square:
        for peer in (core, side, up, after, before):
            greet({"ctx": peer})
        greeted = 5
    else:
        @pl.loop(1, n_ctx)
        def _(by):
            greet({"ctx": lax.rem(me + by, n_ctx)})
        greeted = n_ctx - 1

    @pl.when(z < n_tp - 1)
    def _():
        greet({"tp": z + 1})

    @pl.when(z > 0)
    def _():
        greet({"tp": z - 1})

    first = rows - reach

    def bring(n, source, target):
        copy = pltpu.make_async_copy(source, target, local_sem.at[n])
        copy.start()
        return copy

    later = pl.ds(first, reach)
    get_short = bring(0, short_hbm, short)
    get_tail = bring(1, proj_hbm.at[1:3, later, :], proj.at[1:3, later, :])
    get_head = bring(2, proj_hbm.at[1:3, 0:first, :], proj.at[1:3, 0:first, :])
    get_query = bring(3, proj_hbm.at[0], proj.at[0])
    get_medium = bring(4, medium_hbm, medium)
    get_tables = bring(5, tables_hbm, tables32)
    get_rest = [bring(6, skip_hbm, skip), bring(7, residual_hbm, residual)]
    fwd_hi, fwd_lo = tables.at[0, 0:length, :], tables.at[1, 0:length, :]
    inv_hi, inv_lo = tables.at[0, pl.ds(length, rows), :], tables.at[1, pl.ds(length, rows), :]

    def columns(q):
        return pl.ds(pl.multiple_of(q * WIDE, WIDE), WIDE)

    def edge_copy():
        return pltpu.make_async_remote_copy(
            src_ref=proj_hbm.at[:, pl.ds(rows - EDGE, EDGE), :], dst_ref=edge,
            send_sem=edge_send, recv_sem=edge_recv, device_id={"ctx": after}, device_id_type=MESH)

    def tail_copy(q):
        return pltpu.make_async_remote_copy(
            src_ref=product.at[pl.ds(rows, reach), columns(q)],
            dst_ref=product.at[pl.ds(0, reach), columns(q)],
            send_sem=tail_send.at[q], recv_sem=tail_recv.at[q],
            device_id={"ctx": after}, device_id_type=MESH)

    def z_copy(way, step, q, origin):
        return pltpu.make_async_remote_copy(
            src_ref=gated.at[origin, q], dst_ref=gated.at[origin, q],
            send_sem=z_send.at[way, step, q], recv_sem=z_recv.at[way, step, q],
            device_id={"tp": z + 1 if way == 0 else z - 1}, device_id_type=MESH)

    def z_sends(step, q, act):
        @pl.when((z < n_tp - 1) & (z >= step))
        def _():
            act(z_copy(0, step, q, z - step))

        @pl.when((z > 0) & (z + step <= n_tp - 1))
        def _():
            act(z_copy(1, step, q, z + step))

    def z_wait(step, q):
        @pl.when(z - 1 - step >= 0)
        def _():
            z_copy(0, step, q, z - 1 - step).wait_recv()

        @pl.when(z + 1 + step <= n_tp - 1)
        def _():
            z_copy(1, step, q, z + 1 + step).wait_recv()

    def z_pass(step, q):
        z_wait(step, q)
        if step + 1 < n_tp - 1:
            z_sends(step + 1, q, lambda copy: copy.start())

    part = depth // 2

    def w_rows(block, h):
        return pl.ds(pl.multiple_of(block * depth + h * part, part), part)

    def w_copy(slot, block, h, to, own=False):
        return pltpu.make_async_remote_copy(
            src_ref=weight.at[pl.ds(h * part, part), :] if own else whole.at[w_rows(block, h), :],
            dst_ref=whole.at[w_rows(block, h), :],
            send_sem=w_send.at[slot], recv_sem=w_recv.at[slot],
            device_id={"ctx": to}, device_id_type=MESH)

    def w_all(by):
        return pltpu.make_async_remote_copy(
            src_ref=weight, dst_ref=whole.at[pl.ds(pl.multiple_of(me * depth, depth), depth), :],
            send_sem=w_send.at[by], recv_sem=w_recv.at[by],
            device_id={"ctx": lax.rem(me + by, n_ctx)}, device_id_type=MESH)

    own = pltpu.make_async_copy(
        weight, whole.at[pl.ds(pl.multiple_of(me * depth, depth), depth), :], own_sem)

    def mixed(stream, start, count, cols):
        acc = None
        for j in range(taps):
            term = short32[stream, j : j + 1, cols] * wide[stream, pl.ds(EDGE + start - j, count), cols]
            acc = term if acc is None else acc + term
        return acc

    def multiply(start, count, cols):
        product[pl.ds(reach + start, count), cols] = (
            mixed(1, start, count, cols) * mixed(2, start, count, cols)
        ).astype(jnp.bfloat16)

    def widen(stream, start, count, cols):
        wide[stream, pl.ds(EDGE + start, count), cols] = proj[stream, pl.ds(start, count), cols].astype(jnp.float32)

    def before_edge(q):
        cols = columns(q)
        for stream in (1, 2):
            widen(stream, 0, first, cols)
        widen(0, 0, rows, cols)
        spots = [(EDGE, STEP - EDGE)] + [(start, STEP) for start in range(STEP, rows, STEP)]
        for start, count in spots:
            if start < first:
                multiply(start, count, cols)
            query[pl.ds(start, count), :] = mixed(0, start, count, cols)

    get_short.wait()
    for stream in range(3):
        short32[stream, 0:taps, :] = short[stream].astype(jnp.float32)
    get_tail.wait()
    get_head.wait()

    @pl.loop(0, chunks)
    def _(q):
        cols = columns(q)
        for stream in (1, 2):
            widen(stream, first - EDGE, reach + EDGE, cols)
        for start in range(first, rows, STEP):
            multiply(start, STEP, cols)

    get_tables.wait()

    @pl.loop(0, (length + rows) // 64)
    def _(at):
        span = pl.ds(pl.multiple_of(at * 64, 64), 64)
        value = tables32[span, :]
        high = value.astype(jnp.bfloat16)
        tables[0, span, :] = high
        tables[1, span, :] = (value - high.astype(jnp.float32)).astype(jnp.bfloat16)

    pl.semaphore_wait(barrier, greeted + jnp.where(z < n_tp - 1, 1, 0) + jnp.where(z > 0, 1, 0))
    edge_copy().start()
    for q in range(chunks):
        tail_copy(q).start()
    sent = []
    if square:
        for slot, h, to in ((0, 0, side), (1, 1, up), (2, 1, side), (3, 0, up), (4, 0, core), (5, 1, core)):
            sent.append(w_copy(slot, me, h, to, own=True))
            sent[-1].start()
    else:
        @pl.loop(1, n_ctx)
        def _(by):
            w_all(by).start()
    own.start()

    get_query.wait()
    before_edge(0)

    get_medium.wait()

    @pl.loop(0, chunks)
    def _(q):
        taps_now = medium[:, columns(q)]
        transfer[:, columns(q)] = dot(fwd_hi[:, 0:reach], taps_now) + dot(fwd_lo[:, 0:reach], taps_now)

    for copy in get_rest:
        copy.wait()
    edge_copy().wait_recv()
    for stream in range(3):
        wide[stream, 0:EDGE, :] = jnp.where(me > 0, edge[stream].astype(jnp.float32), 0.0)

    @pl.loop(0, chunks)
    def _(q):
        cols = columns(q)
        multiply(0, EDGE, cols)
        query[0:EDGE, :] = mixed(0, 0, EDGE, cols)
        tail_copy(q).wait_recv()

        @pl.when(me == 0)
        def _():
            product[0:reach, cols] = jnp.zeros((reach, WIDE), jnp.bfloat16)

        window = product[:, cols]
        spec[...] = dot(fwd_hi[...], window) + dot(fwd_lo[...], window)
        for top in range(0, half, 64):
            a, b = spec[top : top + 64, :], spec[half + top : half + top + 64, :]
            c, d = transfer[top : top + 64, cols], transfer[half + top : half + top + 64, cols]
            for at, value in ((top, a * c - b * d), (half + top, a * d + b * c)):
                high = value.astype(jnp.bfloat16)
                spec_hi[at : at + 64, :] = high
                spec_lo[at : at + 64, :] = (value - high.astype(jnp.float32)).astype(jnp.bfloat16)
        filtered = dot(inv_hi[...], spec_hi[...]) + dot(inv_hi[...], spec_lo[...]) + dot(inv_lo[...], spec_hi[...])
        filtered = filtered + skip[:, cols] * product[pl.ds(reach, rows), cols].astype(jnp.float32)
        gated[z, q] = (query[...] * filtered).astype(jnp.bfloat16)
        z_sends(0, q, lambda copy: copy.start())

        @pl.when(q + 1 < chunks)
        def _():
            before_edge(q + 1)

    def project(origin, begin, count):
        @pl.loop(0, outs // WIDE)
        def _(tile):
            cols = columns(tile)
            acc = total[:, cols]
            for q in range(begin, begin + count):
                at = pl.multiple_of(origin * chans + q * WIDE, WIDE)
                acc = acc + dot(gated[origin, q], whole[pl.ds(at, WIDE), cols])
            total[:, cols] = acc

    total[...] = residual[...].astype(jnp.float32)
    for q in range(chunks):
        z_pass(0, q)

    def near(origin):
        return (origin - z <= n_tp - 2) & (z - origin <= n_tp - 2)

    if square:
        far = corner // 2

        def arrived(slot, block, h):
            w_copy(slot, block, h, core).wait_recv()

        def relay(slot, block, h, to):
            copy = w_copy(slot, block, h, to)
            copy.start()
            sent.append(copy)

        arrived(0, side, 0)
        relay(6, side, 0, up)
        relay(8, side, 0, core)
        arrived(1, up, 1)
        relay(7, up, 1, side)
        relay(9, up, 1, core)
        for q in range(chunks // 2):
            z_pass(1, q)
        arrived(2, side, 1)
        relay(10, side, 1, core)
        arrived(3, up, 0)
        relay(11, up, 0, core)
        for q in range(chunks // 2, chunks):
            z_pass(1, q)
        own.wait()
        for slot, block, h in ((4, core, 0), (5, core, 1)):
            arrived(slot, block, h)
        other = core - me
        for slot, block, h in ((8, side, 0), (9, up, 1), (10, side, 1), (11, up, 0)):
            arrived(slot, block + other, h)

        @pl.loop(0, n_tp)
        def _(origin):
            @pl.when(near(origin) & (origin != far))
            def _():
                project(origin, 0, chunks)

        arrived(6, corner, 0)
        relay(12, corner, 0, core)
        arrived(7, corner, 1)
        relay(13, corner, 1, core)
        arrived(12, corner + other, 0)
        arrived(13, corner + other, 1)

        @pl.when(near(far))
        def _():
            project(far, 0, chunks)
    else:
        for step in range(1, n_tp - 2):
            @pl.loop(0, chunks)
            def _(q):
                z_pass(step, q)
        own.wait()

        @pl.loop(1, n_ctx)
        def _(by):
            w_all(by).wait_recv()

        @pl.loop(0, n_tp)
        def _(origin):
            @pl.when(near(origin))
            def _():
                project(origin, 0, chunks)

    for q in range(chunks):
        z_wait(n_tp - 2, q)

        @pl.when((z == 0) | (z == n_tp - 1))
        def _():
            project(n_tp - 1 - z, q, 1)

    out[...] = total[...].astype(jnp.bfloat16)

    edge_copy().wait_send()
    for q in range(chunks):
        tail_copy(q).wait_send()
    if square:
        for copy in sent:
            copy.wait_send()
    else:
        @pl.loop(1, n_ctx)
        def _(by):
            w_all(by).wait_send()
    for step in range(n_tp - 1):
        @pl.loop(0, chunks)
        def _(q):
            z_sends(step, q, lambda copy: copy.wait_send())


def on_device(n_ctx, n_tp, residual, proj, short_filter, medium_filter, skip, out_weight):
    rows, _, chans = proj.shape
    depth, outs = out_weight.shape
    taps, reach = short_filter.shape[0], medium_filter.shape[0]
    length, chunks = rows + reach, chans // WIDE
    tables = jnp.asarray(spectrum_tables(length, reach))
    dma = pltpu.SemaphoreType.DMA
    return pl.pallas_call(
        functools.partial(kernel, n_ctx, n_tp, taps),
        out_shape=jax.ShapeDtypeStruct((rows, outs), jnp.bfloat16),
        in_specs=[pl.BlockSpec(memory_space=pltpu.HBM)] * 7,
        out_specs=pl.BlockSpec(memory_space=pltpu.VMEM),
        scratch_shapes=[
            pltpu.VMEM(residual.shape, residual.dtype),
            pltpu.VMEM((3, rows, chans), proj.dtype),
            pltpu.VMEM((3, taps, chans), short_filter.dtype),
            pltpu.VMEM(medium_filter.shape, medium_filter.dtype),
            pltpu.VMEM((1, chans), skip.dtype),
            pltpu.VMEM(tables.shape, jnp.float32),
            pltpu.VMEM((2,) + tables.shape, jnp.bfloat16),
            pltpu.VMEM((n_ctx * depth, outs), jnp.bfloat16),
            pltpu.VMEM((n_tp, chunks, rows, WIDE), jnp.bfloat16),
            pltpu.VMEM((rows, outs), jnp.float32),
            pltpu.VMEM((3, EDGE + rows, chans), jnp.float32),
            pltpu.VMEM((3, 8, chans), jnp.float32),
            pltpu.VMEM((length, chans), jnp.bfloat16),
            pltpu.VMEM((length, chans), jnp.float32),
            pltpu.VMEM((rows, WIDE), jnp.float32),
            pltpu.VMEM((length, WIDE), jnp.float32),
            pltpu.VMEM((length, WIDE), jnp.bfloat16),
            pltpu.VMEM((length, WIDE), jnp.bfloat16),
            pltpu.VMEM((3, EDGE, chans), jnp.bfloat16),
            dma((8,)),
            dma,
            dma((max(n_ctx, 14),)),
            dma((max(n_ctx, 14),)),
            dma((2, n_tp - 1, chunks)),
            dma((2, n_tp - 1, chunks)),
            dma,
            dma,
            dma((chunks,)),
            dma((chunks,)),
        ],
        compiler_params=pltpu.CompilerParams(
            collective_id=0, has_side_effects=True, vmem_limit_bytes=63 * 2**20
        ),
        cost_estimate=pl.CostEstimate(
            flops=2 * rows * n_ctx * depth * outs, bytes_accessed=2 * rows * chans * 5, transcendentals=0
        ),
    )(
        residual, proj.transpose(1, 0, 2), short_filter.transpose(1, 0, 2), medium_filter,
        skip.reshape(1, chans), out_weight, tables,
    )


def solution(mesh):
    in_specs = (
        P("ctx", "tp"),
        P("ctx", None, "tp"),
        P(None, None, "tp"),
        P(None, "tp"),
        P("tp"),
        P("ctx", "tp"),
    )
    return jax.shard_map(
        functools.partial(on_device, mesh.shape["ctx"], mesh.shape["tp"]),
        mesh=mesh, in_specs=in_specs, out_specs=P("ctx", "tp"), check_vma=False,
    )
```

```python
import functools

import jax
import jax.numpy as jnp
import numpy as np
from jax import lax
from jax.experimental import pallas as pl
from jax.experimental.pallas import tpu as pltpu
from jax.sharding import PartitionSpec as P

WIDE = 256
STEP = 128
PIECES = 8
WINDOW = 6
EDGE = 16
MESH = pl.DeviceIdType.MESH


def spectrum_tables(length, reach):
    half = length // 2
    angle = 2 * np.pi / length * np.outer(np.arange(half) + 0.5, np.arange(length))
    forward = np.concatenate([np.cos(angle), np.sin(angle)], 0)
    inverse = (2.0 / length) * forward.T[reach:]

    return np.concatenate([forward, inverse], 0).astype(np.float32)


def dot(a, b):
    return jnp.dot(a, b, preferred_element_type=jnp.float32)


def kernel(
    n_ctx, n_tp, taps,
    residual_hbm, proj_hbm, short_hbm, medium_hbm, skip_hbm, weight,
    tables_hbm,
    out,
    residual, proj, short, medium, skip, tables32, tables,
    whole, gated, total, wide, short32, product, transfer, query, spec, spec_hi, spec_lo, edge,
    local_sem, own_sem, w_send, w_recv, z_send, z_recv, edge_send, edge_recv, tail_send, tail_recv,
):
    rows, chans = residual.shape[0], proj.shape[2]
    depth, outs = weight.shape
    reach = medium.shape[0]
    chunks = chans // WIDE
    length = rows + reach
    half = length // 2
    me, z = lax.axis_index("ctx"), lax.axis_index("tp")
    after, before = lax.rem(me + 1, n_ctx), lax.rem(me + n_ctx - 1, n_ctx)
    square = n_ctx == 8 and n_tp == 4 and chans == 2 * depth

    def flip(bit):
        return me + bit - 2 * bit * lax.rem(me // bit, 2)

    if square:
        core, side, up = flip(1), flip(2), flip(4)
        corner = side + up - me

    barrier = pltpu.get_barrier_semaphore()

    def greet(where):
        pl.semaphore_signal(barrier, inc=1, device_id=where, device_id_type=MESH)

    if square:
        for peer in (core, side, up, after, before):
            greet({"ctx": peer})
        greeted = 5
    else:
        @pl.loop(1, n_ctx)
        def _(by):
            greet({"ctx": lax.rem(me + by, n_ctx)})
        greeted = n_ctx - 1

    @pl.when(z < n_tp - 1)
    def _():
        greet({"tp": z + 1})

    @pl.when(z > 0)
    def _():
        greet({"tp": z - 1})

    first = rows - reach

    def bring(n, source, target):
        copy = pltpu.make_async_copy(source, target, local_sem.at[n])
        copy.start()
        return copy

    later = pl.ds(first, reach)
    get_short = bring(0, short_hbm, short)
    get_tail = bring(1, proj_hbm.at[1:3, later, :], proj.at[1:3, later, :])
    get_head = bring(2, proj_hbm.at[1:3, 0:first, :], proj.at[1:3, 0:first, :])
    get_query = bring(3, proj_hbm.at[0], proj.at[0])
    get_medium = bring(4, medium_hbm, medium)
    get_tables = bring(5, tables_hbm, tables32)
    get_rest = [bring(6, skip_hbm, skip), bring(7, residual_hbm, residual)]
    fwd_hi, fwd_lo = tables.at[0, 0:length, :], tables.at[1, 0:length, :]
    inv_hi, inv_lo = tables.at[0, pl.ds(length, rows), :], tables.at[1, pl.ds(length, rows), :]

    def columns(q):
        return pl.ds(pl.multiple_of(q * WIDE, WIDE), WIDE)

    def edge_copy():
        return pltpu.make_async_remote_copy(
            src_ref=proj_hbm.at[:, pl.ds(rows - EDGE, EDGE), :], dst_ref=edge,
            send_sem=edge_send, recv_sem=edge_recv, device_id={"ctx": after}, device_id_type=MESH)

    def tail_copy(q):
        return pltpu.make_async_remote_copy(
            src_ref=product.at[pl.ds(rows, reach), columns(q)],
            dst_ref=product.at[pl.ds(0, reach), columns(q)],
            send_sem=tail_send.at[q], recv_sem=tail_recv.at[q],
            device_id={"ctx": after}, device_id_type=MESH)

    def z_copy(way, step, q, origin):
        return pltpu.make_async_remote_copy(
            src_ref=gated.at[origin, q], dst_ref=gated.at[origin, q],
            send_sem=z_send.at[way, step, q], recv_sem=z_recv.at[way, step, q],
            device_id={"tp": z + 1 if way == 0 else z - 1}, device_id_type=MESH)

    def z_sends(step, q, act):
        @pl.when((z < n_tp - 1) & (z >= step))
        def _():
            act(z_copy(0, step, q, z - step))

        @pl.when((z > 0) & (z + step <= n_tp - 1))
        def _():
            act(z_copy(1, step, q, z + step))

    def z_wait(step, q):
        @pl.when(z - 1 - step >= 0)
        def _():
            z_copy(0, step, q, z - 1 - step).wait_recv()

        @pl.when(z + 1 + step <= n_tp - 1)
        def _():
            z_copy(1, step, q, z + 1 + step).wait_recv()

    def z_pass(step, q):
        z_wait(step, q)
        if step + 1 < n_tp - 1:
            z_sends(step + 1, q, lambda copy: copy.start())

    part = depth // PIECES
    to_side = [*range(PIECES)]
    to_up = to_side[PIECES // 2 :] + to_side[: PIECES // 2]
    ticks = PIECES + PIECES // 2

    def w_copy(slot, block, piece, to, own=False):
        rows_there = pl.ds(pl.multiple_of(block * depth + piece * part, part), part)
        return pltpu.make_async_remote_copy(
            src_ref=weight.at[pl.ds(piece * part, part), :] if own else whole.at[rows_there, :],
            dst_ref=whole.at[rows_there, :],
            send_sem=w_send.at[slot], recv_sem=w_recv.at[slot],
            device_id={"ctx": to}, device_id_type=MESH)

    sent = []

    def launch(copy):
        copy.start()
        sent.append(copy)

    def w_tick(t):
        if t < PIECES:
            launch(w_copy(t, me, to_side[t], side, own=True))
            launch(w_copy(ticks + t, me, to_up[t], up, own=True))
        else:
            launch(w_copy(t, up, to_up[t - PIECES], side))
            launch(w_copy(ticks + t, side, to_side[t - PIECES], up))

    def w_come(t):
        if t < PIECES:
            return (t, side, to_side[t]), (ticks + t, up, to_up[t])
        return (t, corner, to_up[t - PIECES]), (ticks + t, corner, to_side[t - PIECES])

    def w_take(t):
        for slot, block, piece in w_come(t):
            w_copy(slot, block, piece, side if slot < ticks else up).wait_recv()
            launch(w_copy(2 * ticks + slot, block, piece, core))

    def w_core(t):
        for slot, block, piece in w_come(t):
            w_copy(2 * ticks + slot, block + core - me, piece, core).wait_recv()

    def w_all(by):
        return pltpu.make_async_remote_copy(
            src_ref=weight, dst_ref=whole.at[pl.ds(pl.multiple_of(me * depth, depth), depth), :],
            send_sem=w_send.at[by], recv_sem=w_recv.at[by],
            device_id={"ctx": lax.rem(me + by, n_ctx)}, device_id_type=MESH)

    own = pltpu.make_async_copy(
        weight, whole.at[pl.ds(pl.multiple_of(me * depth, depth), depth), :], own_sem)

    def mixed(stream, start, count, cols):
        acc = None
        for j in range(taps):
            term = short32[stream, j : j + 1, cols] * wide[stream, pl.ds(EDGE + start - j, count), cols]
            acc = term if acc is None else acc + term
        return acc

    def multiply(start, count, cols):
        product[pl.ds(reach + start, count), cols] = (
            mixed(1, start, count, cols) * mixed(2, start, count, cols)
        ).astype(jnp.bfloat16)

    def widen(stream, start, count, cols):
        wide[stream, pl.ds(EDGE + start, count), cols] = proj[stream, pl.ds(start, count), cols].astype(jnp.float32)

    def before_edge(q):
        cols = columns(q)
        for stream in (1, 2):
            widen(stream, 0, first, cols)
        widen(0, 0, rows, cols)
        spots = [(EDGE, STEP - EDGE)] + [(start, STEP) for start in range(STEP, rows, STEP)]
        for start, count in spots:
            if start < first:
                multiply(start, count, cols)
            query[pl.ds(start, count), :] = mixed(0, start, count, cols)

    get_short.wait()
    for stream in range(3):
        short32[stream, 0:taps, :] = short[stream].astype(jnp.float32)
    get_tail.wait()
    get_head.wait()

    @pl.loop(0, chunks)
    def _(q):
        cols = columns(q)
        for stream in (1, 2):
            widen(stream, first - EDGE, reach + EDGE, cols)
        for start in range(first, rows, STEP):
            multiply(start, STEP, cols)

    get_tables.wait()

    @pl.loop(0, (length + rows) // 64)
    def _(at):
        span = pl.ds(pl.multiple_of(at * 64, 64), 64)
        value = tables32[span, :]
        high = value.astype(jnp.bfloat16)
        tables[0, span, :] = high
        tables[1, span, :] = (value - high.astype(jnp.float32)).astype(jnp.bfloat16)

    pl.semaphore_wait(barrier, greeted + jnp.where(z < n_tp - 1, 1, 0) + jnp.where(z > 0, 1, 0))
    edge_copy().start()
    for q in range(chunks):
        tail_copy(q).start()
    if square:
        for t in range(WINDOW):
            w_tick(t)
        for piece in range(PIECES):
            launch(w_copy(4 * ticks + piece, me, piece, core, own=True))
    else:
        @pl.loop(1, n_ctx)
        def _(by):
            w_all(by).start()
    own.start()

    get_query.wait()
    before_edge(0)

    get_medium.wait()

    @pl.loop(0, chunks)
    def _(q):
        taps_now = medium[:, columns(q)]
        transfer[:, columns(q)] = dot(fwd_hi[:, 0:reach], taps_now) + dot(fwd_lo[:, 0:reach], taps_now)

    for copy in get_rest:
        copy.wait()
    edge_copy().wait_recv()
    for stream in range(3):
        wide[stream, 0:EDGE, :] = jnp.where(me > 0, edge[stream].astype(jnp.float32), 0.0)

    @pl.loop(0, chunks)
    def _(q):
        cols = columns(q)
        multiply(0, EDGE, cols)
        query[0:EDGE, :] = mixed(0, 0, EDGE, cols)
        tail_copy(q).wait_recv()

        @pl.when(me == 0)
        def _():
            product[0:reach, cols] = jnp.zeros((reach, WIDE), jnp.bfloat16)

        window = product[:, cols]
        spec[...] = dot(fwd_hi[...], window) + dot(fwd_lo[...], window)
        for top in range(0, half, 64):
            a, b = spec[top : top + 64, :], spec[half + top : half + top + 64, :]
            c, d = transfer[top : top + 64, cols], transfer[half + top : half + top + 64, cols]
            for at, value in ((top, a * c - b * d), (half + top, a * d + b * c)):
                high = value.astype(jnp.bfloat16)
                spec_hi[at : at + 64, :] = high
                spec_lo[at : at + 64, :] = (value - high.astype(jnp.float32)).astype(jnp.bfloat16)
        filtered = dot(inv_hi[...], spec_hi[...]) + dot(inv_hi[...], spec_lo[...]) + dot(inv_lo[...], spec_hi[...])
        filtered = filtered + skip[:, cols] * product[pl.ds(reach, rows), cols].astype(jnp.float32)
        gated[z, q] = (query[...] * filtered).astype(jnp.bfloat16)
        z_sends(0, q, lambda copy: copy.start())

        @pl.when(q + 1 < chunks)
        def _():
            before_edge(q + 1)

    def project(origin, begin, count):
        @pl.loop(0, outs // WIDE)
        def _(tile):
            cols = columns(tile)
            acc = total[:, cols]
            for q in range(begin, begin + count):
                at = pl.multiple_of(origin * chans + q * WIDE, WIDE)
                acc = acc + dot(gated[origin, q], whole[pl.ds(at, WIDE), cols])
            total[:, cols] = acc

    total[...] = residual[...].astype(jnp.float32)
    def near(origin):
        return (origin - z <= n_tp - 2) & (z - origin <= n_tp - 2)

    if square:
        far = corner // 2
        events = [(step, q) for step in range(n_tp - 2) for q in range(chunks)]
        for t in range(ticks):
            w_take(t)
            if t + WINDOW < ticks:
                w_tick(t + WINDOW)
            if 1 <= t <= len(events):
                z_pass(*events[t - 1])
            if t == len(events):
                own.wait()
                for piece in range(PIECES):
                    w_copy(4 * ticks + piece, core, piece, core).wait_recv()
                for early in range(PIECES):
                    w_core(early)

                @pl.loop(0, n_tp)
                def _(origin):
                    @pl.when(near(origin) & (origin != far))
                    def _():
                        project(origin, 0, chunks)

        for late in range(PIECES, ticks):
            w_core(late)

        @pl.when(near(far))
        def _():
            project(far, 0, chunks)
    else:
        for step in range(n_tp - 2):
            @pl.loop(0, chunks)
            def _(q):
                z_pass(step, q)
        own.wait()

        @pl.loop(1, n_ctx)
        def _(by):
            w_all(by).wait_recv()

        @pl.loop(0, n_tp)
        def _(origin):
            @pl.when(near(origin))
            def _():
                project(origin, 0, chunks)

    for q in range(chunks):
        z_wait(n_tp - 2, q)

        @pl.when((z == 0) | (z == n_tp - 1))
        def _():
            project(n_tp - 1 - z, q, 1)

    out[...] = total[...].astype(jnp.bfloat16)

    edge_copy().wait_send()
    for q in range(chunks):
        tail_copy(q).wait_send()
    if square:
        for copy in sent:
            copy.wait_send()
    else:
        @pl.loop(1, n_ctx)
        def _(by):
            w_all(by).wait_send()
    for step in range(n_tp - 1):
        @pl.loop(0, chunks)
        def _(q):
            z_sends(step, q, lambda copy: copy.wait_send())


def on_device(n_ctx, n_tp, residual, proj, short_filter, medium_filter, skip, out_weight):
    rows, _, chans = proj.shape
    depth, outs = out_weight.shape
    taps, reach = short_filter.shape[0], medium_filter.shape[0]
    length, chunks = rows + reach, chans // WIDE
    tables = jnp.asarray(spectrum_tables(length, reach))
    dma = pltpu.SemaphoreType.DMA
    return pl.pallas_call(
        functools.partial(kernel, n_ctx, n_tp, taps),
        out_shape=jax.ShapeDtypeStruct((rows, outs), jnp.bfloat16),
        in_specs=[pl.BlockSpec(memory_space=pltpu.HBM)] * 7,
        out_specs=pl.BlockSpec(memory_space=pltpu.VMEM),
        scratch_shapes=[
            pltpu.VMEM(residual.shape, residual.dtype),
            pltpu.VMEM((3, rows, chans), proj.dtype),
            pltpu.VMEM((3, taps, chans), short_filter.dtype),
            pltpu.VMEM(medium_filter.shape, medium_filter.dtype),
            pltpu.VMEM((1, chans), skip.dtype),
            pltpu.VMEM(tables.shape, jnp.float32),
            pltpu.VMEM((2,) + tables.shape, jnp.bfloat16),
            pltpu.VMEM((n_ctx * depth, outs), jnp.bfloat16),
            pltpu.VMEM((n_tp, chunks, rows, WIDE), jnp.bfloat16),
            pltpu.VMEM((rows, outs), jnp.float32),
            pltpu.VMEM((3, EDGE + rows, chans), jnp.float32),
            pltpu.VMEM((3, 8, chans), jnp.float32),
            pltpu.VMEM((length, chans), jnp.bfloat16),
            pltpu.VMEM((length, chans), jnp.float32),
            pltpu.VMEM((rows, WIDE), jnp.float32),
            pltpu.VMEM((length, WIDE), jnp.float32),
            pltpu.VMEM((length, WIDE), jnp.bfloat16),
            pltpu.VMEM((length, WIDE), jnp.bfloat16),
            pltpu.VMEM((3, EDGE, chans), jnp.bfloat16),
            dma((8,)),
            dma,
            dma((max(n_ctx, 7 * PIECES),)),
            dma((max(n_ctx, 7 * PIECES),)),
            dma((2, n_tp - 1, chunks)),
            dma((2, n_tp - 1, chunks)),
            dma,
            dma,
            dma((chunks,)),
            dma((chunks,)),
        ],
        compiler_params=pltpu.CompilerParams(
            collective_id=0, has_side_effects=True, vmem_limit_bytes=63 * 2**20
        ),
        cost_estimate=pl.CostEstimate(
            flops=2 * rows * n_ctx * depth * outs, bytes_accessed=2 * rows * chans * 5, transcendentals=0
        ),
    )(
        residual, proj.transpose(1, 0, 2), short_filter.transpose(1, 0, 2), medium_filter,
        skip.reshape(1, chans), out_weight, tables,
    )


def solution(mesh):
    in_specs = (
        P("ctx", "tp"),
        P("ctx", None, "tp"),
        P(None, None, "tp"),
        P(None, "tp"),
        P("tp"),
        P("ctx", "tp"),
    )
    return jax.shard_map(
        functools.partial(on_device, mesh.shape["ctx"], mesh.shape["tp"]),
        mesh=mesh, in_specs=in_specs, out_specs=P("ctx", "tp"), check_vma=False,
    )
```

```python
import functools

import jax
import jax.numpy as jnp
import numpy as np
from jax import lax
from jax.experimental import pallas as pl
from jax.experimental.pallas import tpu as pltpu
from jax.sharding import PartitionSpec as P

WIDE = 256
STEP = 128
PIECES = 8
WINDOW = 6
EDGE = 16
MESH = pl.DeviceIdType.MESH


def spectrum_tables(length, reach):
    half = length // 2
    angle = 2 * np.pi / length * np.outer(np.arange(half) + 0.5, np.arange(length))
    forward = np.concatenate([np.cos(angle), np.sin(angle)], 0)
    inverse = (2.0 / length) * forward.T[reach:]

    return np.concatenate([forward, inverse], 0).astype(np.float32)


def dot(a, b):
    return jnp.dot(a, b, preferred_element_type=jnp.float32)


def kernel(
    n_ctx, n_tp, taps,
    residual_hbm, proj_hbm, short_hbm, medium_hbm, skip_hbm, weight,
    tables_hbm,
    out,
    residual, proj, short, medium, skip, tables32, tables,
    whole, gated, total, wide, short32, product, transfer, query, spec, spec_hi, spec_lo, edge,
    local_sem, own_sem, w_send, w_recv, z_send, z_recv, edge_send, edge_recv, tail_send, tail_recv,
):
    rows, chans = residual.shape[0], proj.shape[2]
    depth, outs = weight.shape
    reach = medium.shape[0]
    chunks = chans // WIDE
    length = rows + reach
    half = length // 2
    me, z = lax.axis_index("ctx"), lax.axis_index("tp")
    after, before = lax.rem(me + 1, n_ctx), lax.rem(me + n_ctx - 1, n_ctx)
    square = n_ctx == 8 and n_tp == 4 and chans == 2 * depth

    def flip(bit):
        return me + bit - 2 * bit * lax.rem(me // bit, 2)

    if square:
        core, side, up = flip(1), flip(2), flip(4)
        corner = side + up - me

    barrier = pltpu.get_barrier_semaphore()

    def greet(where):
        pl.semaphore_signal(barrier, inc=1, device_id=where, device_id_type=MESH)

    if square:
        for peer in (core, side, up, after, before):
            greet({"ctx": peer})
        greeted = 5
    else:
        @pl.loop(1, n_ctx)
        def _(by):
            greet({"ctx": lax.rem(me + by, n_ctx)})
        greeted = n_ctx - 1

    @pl.when(z < n_tp - 1)
    def _():
        greet({"tp": z + 1})

    @pl.when(z > 0)
    def _():
        greet({"tp": z - 1})

    first = rows - reach

    def bring(n, source, target):
        copy = pltpu.make_async_copy(source, target, local_sem.at[n])
        copy.start()
        return copy

    later = pl.ds(first, reach)
    get_short = bring(0, short_hbm, short)
    get_tail = bring(1, proj_hbm.at[1:3, later, :], proj.at[1:3, later, :])
    get_head = bring(2, proj_hbm.at[1:3, 0:first, :], proj.at[1:3, 0:first, :])
    get_query = bring(3, proj_hbm.at[0], proj.at[0])
    get_medium = bring(4, medium_hbm, medium)
    get_tables = bring(5, tables_hbm, tables32)
    get_rest = [bring(6, skip_hbm, skip), bring(7, residual_hbm, residual)]
    fwd_hi, fwd_lo = tables.at[0, 0:length, :], tables.at[1, 0:length, :]
    inv_hi, inv_lo = tables.at[0, pl.ds(length, rows), :], tables.at[1, pl.ds(length, rows), :]

    def columns(q):
        return pl.ds(pl.multiple_of(q * WIDE, WIDE), WIDE)

    def edge_copy():
        return pltpu.make_async_remote_copy(
            src_ref=proj_hbm.at[:, pl.ds(rows - EDGE, EDGE), :], dst_ref=edge,
            send_sem=edge_send, recv_sem=edge_recv, device_id={"ctx": after}, device_id_type=MESH)

    def tail_copy(q):
        return pltpu.make_async_remote_copy(
            src_ref=product.at[pl.ds(rows, reach), columns(q)],
            dst_ref=product.at[pl.ds(0, reach), columns(q)],
            send_sem=tail_send.at[q], recv_sem=tail_recv.at[q],
            device_id={"ctx": after}, device_id_type=MESH)

    def z_copy(way, step, q, origin):
        return pltpu.make_async_remote_copy(
            src_ref=gated.at[origin, q], dst_ref=gated.at[origin, q],
            send_sem=z_send.at[way, step, q], recv_sem=z_recv.at[way, step, q],
            device_id={"tp": z + 1 if way == 0 else z - 1}, device_id_type=MESH)

    def z_sends(step, q, act):
        @pl.when((z < n_tp - 1) & (z >= step))
        def _():
            act(z_copy(0, step, q, z - step))

        @pl.when((z > 0) & (z + step <= n_tp - 1))
        def _():
            act(z_copy(1, step, q, z + step))

    def z_wait(step, q):
        @pl.when(z - 1 - step >= 0)
        def _():
            z_copy(0, step, q, z - 1 - step).wait_recv()

        @pl.when(z + 1 + step <= n_tp - 1)
        def _():
            z_copy(1, step, q, z + 1 + step).wait_recv()

    def z_pass(step, q):
        z_wait(step, q)
        if step + 1 < n_tp - 1:
            z_sends(step + 1, q, lambda copy: copy.start())

    part = depth // PIECES
    to_side = [*range(PIECES)]
    to_up = to_side[PIECES // 2 :] + to_side[: PIECES // 2]
    ticks = PIECES + PIECES // 2

    def w_copy(slot, block, piece, to, own=False):
        rows_there = pl.ds(pl.multiple_of(block * depth + piece * part, part), part)
        return pltpu.make_async_remote_copy(
            src_ref=weight.at[pl.ds(piece * part, part), :] if own else whole.at[rows_there, :],
            dst_ref=whole.at[rows_there, :],
            send_sem=w_send.at[slot], recv_sem=w_recv.at[slot],
            device_id={"ctx": to}, device_id_type=MESH)

    sent = []

    def launch(copy):
        copy.start()
        sent.append(copy)

    def w_tick(t):
        if t < PIECES:
            launch(w_copy(t, me, to_side[t], side, own=True))
            launch(w_copy(ticks + t, me, to_up[t], up, own=True))
        else:
            launch(w_copy(t, up, to_up[t - PIECES], side))
            launch(w_copy(ticks + t, side, to_side[t - PIECES], up))

    def w_come(t):
        if t < PIECES:
            return (t, side, to_side[t]), (ticks + t, up, to_up[t])
        return (t, corner, to_up[t - PIECES]), (ticks + t, corner, to_side[t - PIECES])

    def w_take(t):
        for slot, block, piece in w_come(t):
            w_copy(slot, block, piece, side if slot < ticks else up).wait_recv()
            launch(w_copy(2 * ticks + slot, block, piece, core))

    def w_core(t):
        for slot, block, piece in w_come(t):
            w_copy(2 * ticks + slot, block + core - me, piece, core).wait_recv()

    def w_all(by):
        return pltpu.make_async_remote_copy(
            src_ref=weight, dst_ref=whole.at[pl.ds(pl.multiple_of(me * depth, depth), depth), :],
            send_sem=w_send.at[by], recv_sem=w_recv.at[by],
            device_id={"ctx": lax.rem(me + by, n_ctx)}, device_id_type=MESH)

    own = pltpu.make_async_copy(
        weight, whole.at[pl.ds(pl.multiple_of(me * depth, depth), depth), :], own_sem)

    def mixed(stream, start, count, cols):
        acc = None
        for j in range(taps):
            term = short32[stream, j : j + 1, cols] * wide[stream, pl.ds(EDGE + start - j, count), cols]
            acc = term if acc is None else acc + term
        return acc

    def multiply(start, count, cols):
        product[pl.ds(reach + start, count), cols] = (
            mixed(1, start, count, cols) * mixed(2, start, count, cols)
        ).astype(jnp.bfloat16)

    def widen(stream, start, count, cols):
        wide[stream, pl.ds(EDGE + start, count), cols] = proj[stream, pl.ds(start, count), cols].astype(jnp.float32)

    def before_edge(q):
        cols = columns(q)
        for stream in (1, 2):
            widen(stream, 0, first, cols)
        widen(0, 0, rows, cols)
        spots = [(EDGE, STEP - EDGE)] + [(start, STEP) for start in range(STEP, rows, STEP)]
        for start, count in spots:
            if start < first:
                multiply(start, count, cols)
            query[pl.ds(start, count), :] = mixed(0, start, count, cols)

    get_short.wait()
    for stream in range(3):
        short32[stream, 0:taps, :] = short[stream].astype(jnp.float32)
    get_tail.wait()
    get_head.wait()

    def tail(q):
        cols = columns(q)
        for stream in (1, 2):
            widen(stream, first - EDGE, reach + EDGE, cols)
        for start in range(first, rows, STEP):
            multiply(start, STEP, cols)

    tail(0)
    pl.semaphore_wait(barrier, greeted + jnp.where(z < n_tp - 1, 1, 0) + jnp.where(z > 0, 1, 0))
    edge_copy().start()
    tail_copy(0).start()
    if square:
        for t in range(WINDOW):
            w_tick(t)
        for piece in range(PIECES):
            launch(w_copy(4 * ticks + piece, me, piece, core, own=True))
    else:
        @pl.loop(1, n_ctx)
        def _(by):
            w_all(by).start()
    own.start()

    get_query.wait()
    before_edge(0)

    get_tables.wait()

    @pl.loop(0, (length + rows) // 64)
    def _(at):
        span = pl.ds(pl.multiple_of(at * 64, 64), 64)
        value = tables32[span, :]
        high = value.astype(jnp.bfloat16)
        tables[0, span, :] = high
        tables[1, span, :] = (value - high.astype(jnp.float32)).astype(jnp.bfloat16)

    def spectrum(q):
        taps_now = medium[:, columns(q)]
        transfer[:, columns(q)] = dot(fwd_hi[:, 0:reach], taps_now) + dot(fwd_lo[:, 0:reach], taps_now)

    get_medium.wait()
    spectrum(0)
    for copy in get_rest:
        copy.wait()
    edge_copy().wait_recv()
    for stream in range(3):
        wide[stream, 0:EDGE, :] = jnp.where(me > 0, edge[stream].astype(jnp.float32), 0.0)

    @pl.loop(0, chunks)
    def _(q):
        cols = columns(q)
        multiply(0, EDGE, cols)
        query[0:EDGE, :] = mixed(0, 0, EDGE, cols)
        tail_copy(q).wait_recv()

        @pl.when(me == 0)
        def _():
            product[0:reach, cols] = jnp.zeros((reach, WIDE), jnp.bfloat16)

        window = product[:, cols]
        spec[...] = dot(fwd_hi[...], window) + dot(fwd_lo[...], window)
        for top in range(0, half, 64):
            a, b = spec[top : top + 64, :], spec[half + top : half + top + 64, :]
            c, d = transfer[top : top + 64, cols], transfer[half + top : half + top + 64, cols]
            for at, value in ((top, a * c - b * d), (half + top, a * d + b * c)):
                high = value.astype(jnp.bfloat16)
                spec_hi[at : at + 64, :] = high
                spec_lo[at : at + 64, :] = (value - high.astype(jnp.float32)).astype(jnp.bfloat16)
        filtered = dot(inv_hi[...], spec_hi[...]) + dot(inv_hi[...], spec_lo[...]) + dot(inv_lo[...], spec_hi[...])
        filtered = filtered + skip[:, cols] * product[pl.ds(reach, rows), cols].astype(jnp.float32)
        gated[z, q] = (query[...] * filtered).astype(jnp.bfloat16)
        z_sends(0, q, lambda copy: copy.start())

        @pl.when(q == 0)
        def _():
            @pl.loop(1, chunks)
            def _(other):
                tail(other)
                tail_copy(other).start()

            @pl.loop(1, chunks)
            def _(other):
                spectrum(other)

        @pl.when(q + 1 < chunks)
        def _():
            before_edge(q + 1)

    def project(origin, begin, count):
        @pl.loop(0, outs // WIDE)
        def _(tile):
            cols = columns(tile)
            acc = total[:, cols]
            for q in range(begin, begin + count):
                at = pl.multiple_of(origin * chans + q * WIDE, WIDE)
                acc = acc + dot(gated[origin, q], whole[pl.ds(at, WIDE), cols])
            total[:, cols] = acc

    total[...] = residual[...].astype(jnp.float32)
    def near(origin):
        return (origin - z <= n_tp - 2) & (z - origin <= n_tp - 2)

    if square:
        far = corner // 2
        events = [(step, q) for step in range(n_tp - 2) for q in range(chunks)]
        for t in range(ticks):
            w_take(t)
            if t + WINDOW < ticks:
                w_tick(t + WINDOW)
            if 1 <= t <= len(events):
                z_pass(*events[t - 1])
            if t == len(events):
                own.wait()
                for piece in range(PIECES):
                    w_copy(4 * ticks + piece, core, piece, core).wait_recv()
                for early in range(PIECES):
                    w_core(early)

                @pl.loop(0, n_tp)
                def _(origin):
                    @pl.when(near(origin) & (origin != far))
                    def _():
                        project(origin, 0, chunks)

        for late in range(PIECES, ticks):
            w_core(late)

        @pl.when(near(far))
        def _():
            project(far, 0, chunks)
    else:
        for step in range(n_tp - 2):
            @pl.loop(0, chunks)
            def _(q):
                z_pass(step, q)
        own.wait()

        @pl.loop(1, n_ctx)
        def _(by):
            w_all(by).wait_recv()

        @pl.loop(0, n_tp)
        def _(origin):
            @pl.when(near(origin))
            def _():
                project(origin, 0, chunks)

    for q in range(chunks):
        z_wait(n_tp - 2, q)

        @pl.when((z == 0) | (z == n_tp - 1))
        def _():
            project(n_tp - 1 - z, q, 1)

    out[...] = total[...].astype(jnp.bfloat16)

    edge_copy().wait_send()
    for q in range(chunks):
        tail_copy(q).wait_send()
    if square:
        for copy in sent:
            copy.wait_send()
    else:
        @pl.loop(1, n_ctx)
        def _(by):
            w_all(by).wait_send()
    for step in range(n_tp - 1):
        @pl.loop(0, chunks)
        def _(q):
            z_sends(step, q, lambda copy: copy.wait_send())


def on_device(n_ctx, n_tp, residual, proj, short_filter, medium_filter, skip, out_weight):
    rows, _, chans = proj.shape
    depth, outs = out_weight.shape
    taps, reach = short_filter.shape[0], medium_filter.shape[0]
    length, chunks = rows + reach, chans // WIDE
    tables = jnp.asarray(spectrum_tables(length, reach))
    dma = pltpu.SemaphoreType.DMA
    return pl.pallas_call(
        functools.partial(kernel, n_ctx, n_tp, taps),
        out_shape=jax.ShapeDtypeStruct((rows, outs), jnp.bfloat16),
        in_specs=[pl.BlockSpec(memory_space=pltpu.HBM)] * 7,
        out_specs=pl.BlockSpec(memory_space=pltpu.VMEM),
        scratch_shapes=[
            pltpu.VMEM(residual.shape, residual.dtype),
            pltpu.VMEM((3, rows, chans), proj.dtype),
            pltpu.VMEM((3, taps, chans), short_filter.dtype),
            pltpu.VMEM(medium_filter.shape, medium_filter.dtype),
            pltpu.VMEM((1, chans), skip.dtype),
            pltpu.VMEM(tables.shape, jnp.float32),
            pltpu.VMEM((2,) + tables.shape, jnp.bfloat16),
            pltpu.VMEM((n_ctx * depth, outs), jnp.bfloat16),
            pltpu.VMEM((n_tp, chunks, rows, WIDE), jnp.bfloat16),
            pltpu.VMEM((rows, outs), jnp.float32),
            pltpu.VMEM((3, EDGE + rows, chans), jnp.float32),
            pltpu.VMEM((3, 8, chans), jnp.float32),
            pltpu.VMEM((length, chans), jnp.bfloat16),
            pltpu.VMEM((length, chans), jnp.float32),
            pltpu.VMEM((rows, WIDE), jnp.float32),
            pltpu.VMEM((length, WIDE), jnp.float32),
            pltpu.VMEM((length, WIDE), jnp.bfloat16),
            pltpu.VMEM((length, WIDE), jnp.bfloat16),
            pltpu.VMEM((3, EDGE, chans), jnp.bfloat16),
            dma((8,)),
            dma,
            dma((max(n_ctx, 7 * PIECES),)),
            dma((max(n_ctx, 7 * PIECES),)),
            dma((2, n_tp - 1, chunks)),
            dma((2, n_tp - 1, chunks)),
            dma,
            dma,
            dma((chunks,)),
            dma((chunks,)),
        ],
        compiler_params=pltpu.CompilerParams(
            collective_id=0, has_side_effects=True, vmem_limit_bytes=63 * 2**20
        ),
        cost_estimate=pl.CostEstimate(
            flops=2 * rows * n_ctx * depth * outs, bytes_accessed=2 * rows * chans * 5, transcendentals=0
        ),
    )(
        residual, proj.transpose(1, 0, 2), short_filter.transpose(1, 0, 2), medium_filter,
        skip.reshape(1, chans), out_weight, tables,
    )


def solution(mesh):
    in_specs = (
        P("ctx", "tp"),
        P("ctx", None, "tp"),
        P(None, None, "tp"),
        P(None, "tp"),
        P("tp"),
        P("ctx", "tp"),
    )
    return jax.shard_map(
        functools.partial(on_device, mesh.shape["ctx"], mesh.shape["tp"]),
        mesh=mesh, in_specs=in_specs, out_specs=P("ctx", "tp"), check_vma=False,
    )
```

```python
import functools

import jax
import jax.numpy as jnp
import numpy as np
from jax import lax
from jax.experimental import pallas as pl
from jax.experimental.pallas import tpu as pltpu
from jax.sharding import PartitionSpec as P

WIDE = 256
STEP = 64
PIECES = 8
WINDOW = 8
EDGE = 16
MESH = pl.DeviceIdType.MESH


def spectrum_tables(length, reach):
    half = length // 2
    angle = 2 * np.pi / length * np.outer(np.arange(half) + 0.5, np.arange(length))
    forward = np.concatenate([np.cos(angle), np.sin(angle)], 0)
    inverse = (2.0 / length) * forward.T[reach:]

    return np.concatenate([forward, inverse], 0).astype(np.float32)


def dot(a, b):
    return jnp.dot(a, b, preferred_element_type=jnp.float32)


def kernel(
    n_ctx, n_tp, taps,
    residual_hbm, proj_hbm, short_hbm, medium_hbm, skip_hbm, weight,
    tables_hbm,
    out,
    residual, proj, short, medium, skip, tables32, tables,
    whole, gated, total, wide, short32, product, transfer, query, spec, spec_out, edge,
    local_sem, own_sem, w_send, w_recv, z_send, z_recv, edge_send, edge_recv, tail_send, tail_recv,
):
    rows, chans = residual.shape[0], proj.shape[2]
    depth, outs = weight.shape
    reach = medium.shape[0]
    chunks = chans // WIDE
    length = rows + reach
    half = length // 2
    me, z = lax.axis_index("ctx"), lax.axis_index("tp")
    after, before = lax.rem(me + 1, n_ctx), lax.rem(me + n_ctx - 1, n_ctx)
    square = n_ctx == 8 and n_tp == 4 and chans == 2 * depth

    def flip(bit):
        return me + bit - 2 * bit * lax.rem(me // bit, 2)

    if square:
        core, side, up = flip(1), flip(2), flip(4)
        corner = side + up - me

    barrier = pltpu.get_barrier_semaphore()

    def greet(where):
        pl.semaphore_signal(barrier, inc=1, device_id=where, device_id_type=MESH)

    if square:
        for peer in (core, side, up, after, before):
            greet({"ctx": peer})
        greeted = 5
    else:
        @pl.loop(1, n_ctx)
        def _(by):
            greet({"ctx": lax.rem(me + by, n_ctx)})
        greeted = n_ctx - 1

    @pl.when(z < n_tp - 1)
    def _():
        greet({"tp": z + 1})

    @pl.when(z > 0)
    def _():
        greet({"tp": z - 1})

    first = rows - reach

    def bring(n, source, target):
        copy = pltpu.make_async_copy(source, target, local_sem.at[n])
        copy.start()
        return copy

    later = pl.ds(first, reach)
    get_short = bring(0, short_hbm, short)
    get_tail = bring(1, proj_hbm.at[1:3, later, :], proj.at[1:3, later, :])
    get_head = bring(2, proj_hbm.at[1:3, 0:first, :], proj.at[1:3, 0:first, :])
    get_query = bring(3, proj_hbm.at[0], proj.at[0])
    get_medium = bring(4, medium_hbm, medium)
    get_tables = bring(5, tables_hbm, tables32)
    get_rest = [bring(6, skip_hbm, skip), bring(7, residual_hbm, residual)]
    forward, inverse = tables.at[0:length, :], tables.at[pl.ds(length, rows), :]

    def columns(q):
        return pl.ds(pl.multiple_of(q * WIDE, WIDE), WIDE)

    def edge_copy():
        return pltpu.make_async_remote_copy(
            src_ref=proj_hbm.at[:, pl.ds(rows - EDGE, EDGE), :], dst_ref=edge,
            send_sem=edge_send, recv_sem=edge_recv, device_id={"ctx": after}, device_id_type=MESH)

    def tail_copy(q):
        return pltpu.make_async_remote_copy(
            src_ref=product.at[pl.ds(rows, reach), columns(q)],
            dst_ref=product.at[pl.ds(0, reach), columns(q)],
            send_sem=tail_send.at[q], recv_sem=tail_recv.at[q],
            device_id={"ctx": after}, device_id_type=MESH)

    def z_copy(way, step, q, origin):
        return pltpu.make_async_remote_copy(
            src_ref=gated.at[origin, q], dst_ref=gated.at[origin, q],
            send_sem=z_send.at[way, step, q], recv_sem=z_recv.at[way, step, q],
            device_id={"tp": z + 1 if way == 0 else z - 1}, device_id_type=MESH)

    def z_sends(step, q, act):
        @pl.when((z < n_tp - 1) & (z >= step))
        def _():
            act(z_copy(0, step, q, z - step))

        @pl.when((z > 0) & (z + step <= n_tp - 1))
        def _():
            act(z_copy(1, step, q, z + step))

    def z_wait(step, q):
        @pl.when(z - 1 - step >= 0)
        def _():
            z_copy(0, step, q, z - 1 - step).wait_recv()

        @pl.when(z + 1 + step <= n_tp - 1)
        def _():
            z_copy(1, step, q, z + 1 + step).wait_recv()

    def z_pass(step, q):
        z_wait(step, q)
        if step + 1 < n_tp - 1:
            z_sends(step + 1, q, lambda copy: copy.start())

    part = depth // PIECES
    to_side = [*range(PIECES)]
    to_up = to_side[PIECES // 2 :] + to_side[: PIECES // 2]
    ticks = PIECES + PIECES // 2

    def w_copy(slot, block, piece, to, own=False):
        rows_there = pl.ds(pl.multiple_of(block * depth + piece * part, part), part)
        return pltpu.make_async_remote_copy(
            src_ref=weight.at[pl.ds(piece * part, part), :] if own else whole.at[rows_there, :],
            dst_ref=whole.at[rows_there, :],
            send_sem=w_send.at[slot], recv_sem=w_recv.at[slot],
            device_id={"ctx": to}, device_id_type=MESH)

    sent = []

    def launch(copy):
        copy.start()
        sent.append(copy)

    def w_tick(t):
        if t < PIECES:
            launch(w_copy(t, me, to_side[t], side, own=True))
            launch(w_copy(ticks + t, me, to_up[t], up, own=True))
        else:
            launch(w_copy(t, up, to_up[t - PIECES], side))
            launch(w_copy(ticks + t, side, to_side[t - PIECES], up))

    def w_come(t):
        if t < PIECES:
            return (t, side, to_side[t]), (ticks + t, up, to_up[t])
        return (t, corner, to_up[t - PIECES]), (ticks + t, corner, to_side[t - PIECES])

    def w_take(t):
        for slot, block, piece in w_come(t):
            w_copy(slot, block, piece, side if slot < ticks else up).wait_recv()
            launch(w_copy(2 * ticks + slot, block, piece, core))

    def w_core(t):
        for slot, block, piece in w_come(t):
            w_copy(2 * ticks + slot, block + core - me, piece, core).wait_recv()

    def w_all(by):
        return pltpu.make_async_remote_copy(
            src_ref=weight, dst_ref=whole.at[pl.ds(pl.multiple_of(me * depth, depth), depth), :],
            send_sem=w_send.at[by], recv_sem=w_recv.at[by],
            device_id={"ctx": lax.rem(me + by, n_ctx)}, device_id_type=MESH)

    own = pltpu.make_async_copy(
        weight, whole.at[pl.ds(pl.multiple_of(me * depth, depth), depth), :], own_sem)

    def mixed(stream, start, count, cols):
        acc = None
        for j in range(taps):
            term = short32[stream, j : j + 1, cols] * wide[stream, pl.ds(EDGE + start - j, count), cols]
            acc = term if acc is None else acc + term
        return acc

    def multiply(start, count, cols):
        product[pl.ds(reach + start, count), cols] = (
            mixed(1, start, count, cols) * mixed(2, start, count, cols)
        ).astype(jnp.bfloat16)

    def widen(stream, start, count, cols):
        wide[stream, pl.ds(EDGE + start, count), cols] = proj[stream, pl.ds(start, count), cols].astype(jnp.float32)

    def before_edge(q):
        cols = columns(q)
        for stream in (1, 2):
            widen(stream, 0, first, cols)
        widen(0, 0, rows, cols)
        spots = [(EDGE, STEP - EDGE)] + [(start, STEP) for start in range(STEP, rows, STEP)]
        for start, count in spots:
            if start < first:
                multiply(start, count, cols)
            query[pl.ds(start, count), :] = mixed(0, start, count, cols)

    get_short.wait()
    for stream in range(3):
        short32[stream, 0:taps, :] = short[stream].astype(jnp.float32)
    get_tail.wait()
    get_head.wait()

    @pl.loop(0, chunks)
    def _(q):
        cols = columns(q)
        for stream in (1, 2):
            widen(stream, first - EDGE, reach + EDGE, cols)
        for start in range(first, rows, STEP):
            multiply(start, STEP, cols)

    get_tables.wait()

    @pl.loop(0, (length + rows) // 64)
    def _(at):
        span = pl.ds(pl.multiple_of(at * 64, 64), 64)
        tables[span, :] = tables32[span, :].astype(jnp.bfloat16)

    pl.semaphore_wait(barrier, greeted + jnp.where(z < n_tp - 1, 1, 0) + jnp.where(z > 0, 1, 0))
    edge_copy().start()
    for q in range(chunks):
        tail_copy(q).start()
    if square:
        for t in range(WINDOW):
            w_tick(t)
        for piece in range(PIECES):
            launch(w_copy(4 * ticks + piece, me, piece, core, own=True))
    else:
        @pl.loop(1, n_ctx)
        def _(by):
            w_all(by).start()
    own.start()

    get_query.wait()
    before_edge(0)

    get_medium.wait()

    @pl.loop(0, chunks)
    def _(q):
        taps_now = medium[:, columns(q)]
        transfer[:, columns(q)] = dot(forward[:, 0:reach], taps_now)

    for copy in get_rest:
        copy.wait()
    edge_copy().wait_recv()
    for stream in range(3):
        wide[stream, 0:EDGE, :] = jnp.where(me > 0, edge[stream].astype(jnp.float32), 0.0)

    @pl.loop(0, chunks)
    def _(q):
        cols = columns(q)
        multiply(0, EDGE, cols)
        query[0:EDGE, :] = mixed(0, 0, EDGE, cols)
        tail_copy(q).wait_recv()

        @pl.when(me == 0)
        def _():
            product[0:reach, cols] = jnp.zeros((reach, WIDE), jnp.bfloat16)

        window = product[:, cols]
        spec[...] = dot(forward[...], window)
        for top in range(0, half, 64):
            a, b = spec[top : top + 64, :], spec[half + top : half + top + 64, :]
            c, d = transfer[top : top + 64, cols], transfer[half + top : half + top + 64, cols]
            for at, value in ((top, a * c - b * d), (half + top, a * d + b * c)):
                spec_out[at : at + 64, :] = value.astype(jnp.bfloat16)
        filtered = dot(inverse[...], spec_out[...])
        filtered = filtered + skip[:, cols] * product[pl.ds(reach, rows), cols].astype(jnp.float32)
        gated[z, q] = (query[...] * filtered).astype(jnp.bfloat16)
        z_sends(0, q, lambda copy: copy.start())

        @pl.when(q + 1 < chunks)
        def _():
            before_edge(q + 1)

    def project(origin, begin, count):
        @pl.loop(0, outs // WIDE)
        def _(tile):
            cols = columns(tile)
            acc = total[:, cols]
            for q in range(begin, begin + count):
                at = pl.multiple_of(origin * chans + q * WIDE, WIDE)
                acc = acc + dot(gated[origin, q], whole[pl.ds(at, WIDE), cols])
            total[:, cols] = acc

    total[...] = residual[...].astype(jnp.float32)
    def near(origin):
        return (origin - z <= n_tp - 2) & (z - origin <= n_tp - 2)

    if square:
        far = corner // 2
        events = [(step, q) for step in range(n_tp - 2) for q in range(chunks)]
        for t in range(ticks):
            w_take(t)
            if t + WINDOW < ticks:
                w_tick(t + WINDOW)
            if 1 <= t <= len(events):
                z_pass(*events[t - 1])
            if t == len(events):
                own.wait()
                for piece in range(PIECES):
                    w_copy(4 * ticks + piece, core, piece, core).wait_recv()
                for early in range(PIECES):
                    w_core(early)

                @pl.loop(0, n_tp)
                def _(origin):
                    @pl.when(near(origin) & (origin != far))
                    def _():
                        project(origin, 0, chunks)

        for late in range(PIECES, ticks):
            w_core(late)

        @pl.when(near(far))
        def _():
            project(far, 0, chunks)
    else:
        for step in range(n_tp - 2):
            @pl.loop(0, chunks)
            def _(q):
                z_pass(step, q)
        own.wait()

        @pl.loop(1, n_ctx)
        def _(by):
            w_all(by).wait_recv()

        @pl.loop(0, n_tp)
        def _(origin):
            @pl.when(near(origin))
            def _():
                project(origin, 0, chunks)

    for q in range(chunks):
        z_wait(n_tp - 2, q)

        @pl.when((z == 0) | (z == n_tp - 1))
        def _():
            project(n_tp - 1 - z, q, 1)

    out[...] = total[...].astype(jnp.bfloat16)

    edge_copy().wait_send()
    for q in range(chunks):
        tail_copy(q).wait_send()
    if square:
        for copy in sent:
            copy.wait_send()
    else:
        @pl.loop(1, n_ctx)
        def _(by):
            w_all(by).wait_send()
    for step in range(n_tp - 1):
        @pl.loop(0, chunks)
        def _(q):
            z_sends(step, q, lambda copy: copy.wait_send())


def on_device(n_ctx, n_tp, residual, proj, short_filter, medium_filter, skip, out_weight):
    rows, _, chans = proj.shape
    depth, outs = out_weight.shape
    taps, reach = short_filter.shape[0], medium_filter.shape[0]
    length, chunks = rows + reach, chans // WIDE
    tables = jnp.asarray(spectrum_tables(length, reach))
    dma = pltpu.SemaphoreType.DMA
    return pl.pallas_call(
        functools.partial(kernel, n_ctx, n_tp, taps),
        out_shape=jax.ShapeDtypeStruct((rows, outs), jnp.bfloat16),
        in_specs=[pl.BlockSpec(memory_space=pltpu.HBM)] * 7,
        out_specs=pl.BlockSpec(memory_space=pltpu.VMEM),
        scratch_shapes=[
            pltpu.VMEM(residual.shape, residual.dtype),
            pltpu.VMEM((3, rows, chans), proj.dtype),
            pltpu.VMEM((3, taps, chans), short_filter.dtype),
            pltpu.VMEM(medium_filter.shape, medium_filter.dtype),
            pltpu.VMEM((1, chans), skip.dtype),
            pltpu.VMEM(tables.shape, jnp.float32),
            pltpu.VMEM(tables.shape, jnp.bfloat16),
            pltpu.VMEM((n_ctx * depth, outs), jnp.bfloat16),
            pltpu.VMEM((n_tp, chunks, rows, WIDE), jnp.bfloat16),
            pltpu.VMEM((rows, outs), jnp.float32),
            pltpu.VMEM((3, EDGE + rows, chans), jnp.float32),
            pltpu.VMEM((3, 8, chans), jnp.float32),
            pltpu.VMEM((length, chans), jnp.bfloat16),
            pltpu.VMEM((length, chans), jnp.float32),
            pltpu.VMEM((rows, WIDE), jnp.float32),
            pltpu.VMEM((length, WIDE), jnp.float32),
            pltpu.VMEM((length, WIDE), jnp.bfloat16),
            pltpu.VMEM((3, EDGE, chans), jnp.bfloat16),
            dma((8,)),
            dma,
            dma((max(n_ctx, 7 * PIECES),)),
            dma((max(n_ctx, 7 * PIECES),)),
            dma((2, n_tp - 1, chunks)),
            dma((2, n_tp - 1, chunks)),
            dma,
            dma,
            dma((chunks,)),
            dma((chunks,)),
        ],
        compiler_params=pltpu.CompilerParams(
            collective_id=0, has_side_effects=True, vmem_limit_bytes=44 * 2**20
        ),
        cost_estimate=pl.CostEstimate(
            flops=2 * rows * n_ctx * depth * outs, bytes_accessed=2 * rows * chans * 5, transcendentals=0
        ),
    )(*(
        pltpu.with_memory_space_constraint(array, pltpu.HBM)
        for array in (
            residual, proj.transpose(1, 0, 2), short_filter.transpose(1, 0, 2), medium_filter,
            skip.reshape(1, chans), out_weight, tables,
        )
    ))


def solution(mesh):
    in_specs = (
        P("ctx", "tp"),
        P("ctx", None, "tp"),
        P(None, None, "tp"),
        P(None, "tp"),
        P("tp"),
        P("ctx", "tp"),
    )
    return jax.shard_map(
        functools.partial(on_device, mesh.shape["ctx"], mesh.shape["tp"]),
        mesh=mesh, in_specs=in_specs, out_specs=P("ctx", "tp"), check_vma=False,
    )
```

```python
import functools

import jax
import jax.numpy as jnp
import numpy as np
from jax import lax
from jax.experimental import pallas as pl
from jax.experimental.pallas import tpu as pltpu
from jax.sharding import PartitionSpec as P

WIDE = 256
STEP = 64
PIECES = 8
WINDOW = 6
EDGE = 16
MESH = pl.DeviceIdType.MESH


def spectrum_tables(length, reach):
    half = length // 2
    angle = 2 * np.pi / length * np.outer(np.arange(half) + 0.5, np.arange(length))
    forward = np.concatenate([np.cos(angle), np.sin(angle)], 0)
    inverse = (2.0 / length) * forward.T[reach:]

    return np.concatenate([forward, inverse], 0).astype(np.float32)


def dot(a, b):
    return jnp.dot(a, b, preferred_element_type=jnp.float32)


def kernel(
    n_ctx, n_tp, taps,
    residual_hbm, proj_hbm, short_hbm, medium_hbm, skip_hbm, weight,
    tables_hbm,
    out,
    residual, proj, short, medium, skip, tables32, tables,
    whole, gated, total, wide, short32, product, transfer, query, spec, spec_out, edge,
    local_sem, own_sem, w_send, w_recv, z_send, z_recv, edge_send, edge_recv, tail_send, tail_recv,
):
    rows, chans = residual.shape[0], proj.shape[2]
    depth, outs = weight.shape
    reach = medium.shape[0]
    chunks = chans // WIDE
    length = rows + reach
    half = length // 2
    me, z = lax.axis_index("ctx"), lax.axis_index("tp")
    after, before = lax.rem(me + 1, n_ctx), lax.rem(me + n_ctx - 1, n_ctx)
    square = n_ctx == 8 and n_tp == 4 and chans == 2 * depth

    def flip(bit):
        return me + bit - 2 * bit * lax.rem(me // bit, 2)

    if square:
        core, side, up = flip(1), flip(2), flip(4)
        corner = side + up - me

    barrier = pltpu.get_barrier_semaphore()

    def greet(where):
        pl.semaphore_signal(barrier, inc=1, device_id=where, device_id_type=MESH)

    if square:
        for peer in (core, side, up, after, before):
            greet({"ctx": peer})
        greeted = 5
    else:
        @pl.loop(1, n_ctx)
        def _(by):
            greet({"ctx": lax.rem(me + by, n_ctx)})
        greeted = n_ctx - 1

    @pl.when(z < n_tp - 1)
    def _():
        greet({"tp": z + 1})

    @pl.when(z > 0)
    def _():
        greet({"tp": z - 1})

    first = rows - reach

    def bring(n, source, target):
        copy = pltpu.make_async_copy(source, target, local_sem.at[n])
        copy.start()
        return copy

    later = pl.ds(first, reach)
    get_short = bring(0, short_hbm, short)
    get_tail = bring(1, proj_hbm.at[1:3, later, :], proj.at[1:3, later, :])
    get_head = bring(2, proj_hbm.at[1:3, 0:first, :], proj.at[1:3, 0:first, :])
    get_query = bring(3, proj_hbm.at[0], proj.at[0])
    get_medium = bring(4, medium_hbm, medium)
    get_tables = bring(5, tables_hbm, tables32)
    get_rest = [bring(6, skip_hbm, skip), bring(7, residual_hbm, residual)]
    forward, inverse = tables.at[0:length, :], tables.at[pl.ds(length, rows), :]

    def columns(q):
        return pl.ds(pl.multiple_of(q * WIDE, WIDE), WIDE)

    def edge_copy():
        return pltpu.make_async_remote_copy(
            src_ref=proj_hbm.at[:, pl.ds(rows - EDGE, EDGE), :], dst_ref=edge,
            send_sem=edge_send, recv_sem=edge_recv, device_id={"ctx": after}, device_id_type=MESH)

    def tail_copy(q):
        return pltpu.make_async_remote_copy(
            src_ref=product.at[pl.ds(rows, reach), columns(q)],
            dst_ref=product.at[pl.ds(0, reach), columns(q)],
            send_sem=tail_send.at[q], recv_sem=tail_recv.at[q],
            device_id={"ctx": after}, device_id_type=MESH)

    cut = reach + EDGE
    spans = [(cut, rows - cut), (0, cut)]

    def z_copy(way, step, piece, origin):
        part_of, q = piece
        there = gated.at[origin, q, pl.ds(*spans[part_of]), :]
        return pltpu.make_async_remote_copy(
            src_ref=there, dst_ref=there,
            send_sem=z_send.at[way, step, part_of, q], recv_sem=z_recv.at[way, step, part_of, q],
            device_id={"tp": z + 1 if way == 0 else z - 1}, device_id_type=MESH)

    def z_sends(step, q, act):
        @pl.when((z < n_tp - 1) & (z >= step))
        def _():
            act(z_copy(0, step, q, z - step))

        @pl.when((z > 0) & (z + step <= n_tp - 1))
        def _():
            act(z_copy(1, step, q, z + step))

    def z_wait(step, q):
        @pl.when(z - 1 - step >= 0)
        def _():
            z_copy(0, step, q, z - 1 - step).wait_recv()

        @pl.when(z + 1 + step <= n_tp - 1)
        def _():
            z_copy(1, step, q, z + 1 + step).wait_recv()

    def z_pass(step, q):
        z_wait(step, q)
        if step + 1 < n_tp - 1:
            z_sends(step + 1, q, lambda copy: copy.start())

    part = depth // PIECES
    to_side = [*range(PIECES)]
    to_up = to_side[PIECES // 2 :] + to_side[: PIECES // 2]
    ticks = PIECES + PIECES // 2

    def w_copy(slot, block, piece, to, own=False):
        rows_there = pl.ds(pl.multiple_of(block * depth + piece * part, part), part)
        return pltpu.make_async_remote_copy(
            src_ref=weight.at[pl.ds(piece * part, part), :] if own else whole.at[rows_there, :],
            dst_ref=whole.at[rows_there, :],
            send_sem=w_send.at[slot], recv_sem=w_recv.at[slot],
            device_id={"ctx": to}, device_id_type=MESH)

    sent = []

    def launch(copy):
        copy.start()
        sent.append(copy)

    def w_tick(t):
        if t < PIECES:
            launch(w_copy(t, me, to_side[t], side, own=True))
            launch(w_copy(ticks + t, me, to_up[t], up, own=True))
        else:
            launch(w_copy(t, up, to_up[t - PIECES], side))
            launch(w_copy(ticks + t, side, to_side[t - PIECES], up))

    def w_come(t):
        if t < PIECES:
            return (t, side, to_side[t]), (ticks + t, up, to_up[t])
        return (t, corner, to_up[t - PIECES]), (ticks + t, corner, to_side[t - PIECES])

    def w_take(t):
        for slot, block, piece in w_come(t):
            w_copy(slot, block, piece, side if slot < ticks else up).wait_recv()
            launch(w_copy(2 * ticks + slot, block, piece, core))

    def w_core(t):
        for slot, block, piece in w_come(t):
            w_copy(2 * ticks + slot, block + core - me, piece, core).wait_recv()

    def w_all(by):
        return pltpu.make_async_remote_copy(
            src_ref=weight, dst_ref=whole.at[pl.ds(pl.multiple_of(me * depth, depth), depth), :],
            send_sem=w_send.at[by], recv_sem=w_recv.at[by],
            device_id={"ctx": lax.rem(me + by, n_ctx)}, device_id_type=MESH)

    own = pltpu.make_async_copy(
        weight, whole.at[pl.ds(pl.multiple_of(me * depth, depth), depth), :], own_sem)

    def mixed(stream, start, count, cols):
        acc = None
        for j in range(taps):
            term = short32[stream, j : j + 1, cols] * wide[stream, pl.ds(EDGE + start - j, count), cols]
            acc = term if acc is None else acc + term
        return acc

    def multiply(start, count, cols):
        product[pl.ds(reach + start, count), cols] = (
            mixed(1, start, count, cols) * mixed(2, start, count, cols)
        ).astype(jnp.bfloat16)

    def widen(stream, start, count, cols):
        wide[stream, pl.ds(EDGE + start, count), cols] = proj[stream, pl.ds(start, count), cols].astype(jnp.float32)

    def before_edge(q):
        cols = columns(q)
        for stream in (1, 2):
            widen(stream, 0, first, cols)
        widen(0, 0, rows, cols)
        spots = [(EDGE, STEP - EDGE)] + [(start, STEP) for start in range(STEP, rows, STEP)]
        for start, count in spots:
            if start < first:
                multiply(start, count, cols)
            query[pl.ds(start, count), cols] = mixed(0, start, count, cols)

    get_short.wait()
    for stream in range(3):
        short32[stream, 0:taps, :] = short[stream].astype(jnp.float32)
    get_tail.wait()
    get_head.wait()

    @pl.loop(0, chunks)
    def _(q):
        cols = columns(q)
        for stream in (1, 2):
            widen(stream, first - EDGE, reach + EDGE, cols)
        for start in range(first, rows, STEP):
            multiply(start, STEP, cols)

    get_tables.wait()

    @pl.loop(0, (length + rows) // 64)
    def _(at):
        span = pl.ds(pl.multiple_of(at * 64, 64), 64)
        tables[span, :] = tables32[span, :].astype(jnp.bfloat16)

    pl.semaphore_wait(barrier, greeted + jnp.where(z < n_tp - 1, 1, 0) + jnp.where(z > 0, 1, 0))
    edge_copy().start()
    for q in range(chunks):
        tail_copy(q).start()
    if square:
        for t in range(WINDOW):
            w_tick(t)
        for piece in range(PIECES):
            launch(w_copy(4 * ticks + piece, me, piece, core, own=True))
    else:
        @pl.loop(1, n_ctx)
        def _(by):
            w_all(by).start()
    own.start()

    get_query.wait()
    before_edge(0)

    get_medium.wait()

    @pl.loop(0, chunks)
    def _(q):
        taps_now = medium[:, columns(q)]
        transfer[:, columns(q)] = dot(forward[:, 0:reach], taps_now)

    for copy in get_rest:
        copy.wait()
    def gate(part_of, q, skipped):
        cols = columns(q)
        start, count = spans[part_of]
        window = product[skipped:, cols]
        spec[...] = dot(forward[:, skipped:], window)
        for top in range(0, half, 64):
            a, b = spec[top : top + 64, :], spec[half + top : half + top + 64, :]
            c, d = transfer[top : top + 64, cols], transfer[half + top : half + top + 64, cols]
            for at, value in ((top, a * c - b * d), (half + top, a * d + b * c)):
                spec_out[at : at + 64, :] = value.astype(jnp.bfloat16)
        filtered = dot(inverse[pl.ds(start, count), :], spec_out[...])
        filtered = filtered + skip[:, cols] * product[pl.ds(reach + start, count), cols].astype(jnp.float32)
        gated[z, q, pl.ds(start, count), :] = (query[pl.ds(start, count), cols] * filtered).astype(jnp.bfloat16)
        z_sends(0, (part_of, q), lambda copy: copy.start())

    @pl.loop(0, chunks)
    def _(q):
        product[pl.ds(reach, EDGE), columns(q)] = jnp.zeros((EDGE, WIDE), jnp.bfloat16)
        gate(0, q, reach)

        @pl.when(q + 1 < chunks)
        def _():
            before_edge(q + 1)

    edge_copy().wait_recv()
    for stream in range(3):
        wide[stream, 0:EDGE, :] = jnp.where(me > 0, edge[stream].astype(jnp.float32), 0.0)

    @pl.loop(0, chunks)
    def _(q):
        cols = columns(q)
        multiply(0, EDGE, cols)
        query[0:EDGE, cols] = mixed(0, 0, EDGE, cols)
        tail_copy(q).wait_recv()

        @pl.when(me == 0)
        def _():
            product[0:reach, cols] = jnp.zeros((reach, WIDE), jnp.bfloat16)

        gate(1, q, 0)

    def project(origin, begin, count):
        @pl.loop(0, outs // WIDE)
        def _(tile):
            cols = columns(tile)
            acc = total[:, cols]
            for q in range(begin, begin + count):
                at = pl.multiple_of(origin * chans + q * WIDE, WIDE)
                acc = acc + dot(gated[origin, q], whole[pl.ds(at, WIDE), cols])
            total[:, cols] = acc

    total[...] = residual[...].astype(jnp.float32)
    def near(origin):
        return (origin - z <= n_tp - 2) & (z - origin <= n_tp - 2)

    if square:
        far = corner // 2
        events = [(step, (part_of, q)) for step in range(n_tp - 2) for part_of in range(2) for q in range(chunks)]
        for t in range(ticks):
            for event in events[2 * t : 2 * t + 2]:
                z_pass(*event)
            w_take(t)
            if t + WINDOW < ticks:
                w_tick(t + WINDOW)
            if t == PIECES:
                own.wait()
                for piece in range(PIECES):
                    w_copy(4 * ticks + piece, core, piece, core).wait_recv()
                for early in range(PIECES):
                    w_core(early)

                @pl.loop(0, n_tp)
                def _(origin):
                    @pl.when(near(origin) & (origin != far))
                    def _():
                        project(origin, 0, chunks)

        for late in range(PIECES, ticks):
            w_core(late)

        @pl.when(near(far))
        def _():
            project(far, 0, chunks)
    else:
        for step in range(n_tp - 2):
            @pl.loop(0, chunks)
            def _(q):
                z_pass(step, (0, q))

            @pl.loop(0, chunks)
            def _(q):
                z_pass(step, (1, q))

        own.wait()

        @pl.loop(1, n_ctx)
        def _(by):
            w_all(by).wait_recv()

        @pl.loop(0, n_tp)
        def _(origin):
            @pl.when(near(origin))
            def _():
                project(origin, 0, chunks)

    for q in range(chunks):
        z_wait(n_tp - 2, (0, q))
    for q in range(chunks):
        z_wait(n_tp - 2, (1, q))

        @pl.when((z == 0) | (z == n_tp - 1))
        def _():
            project(n_tp - 1 - z, q, 1)

    out[...] = total[...].astype(jnp.bfloat16)

    edge_copy().wait_send()
    for q in range(chunks):
        tail_copy(q).wait_send()
    if square:
        for copy in sent:
            copy.wait_send()
    else:
        @pl.loop(1, n_ctx)
        def _(by):
            w_all(by).wait_send()
    for step in range(n_tp - 1):
        @pl.loop(0, chunks)
        def _(q):
            for part_of in range(2):
                z_sends(step, (part_of, q), lambda copy: copy.wait_send())


def on_device(n_ctx, n_tp, residual, proj, short_filter, medium_filter, skip, out_weight):
    rows, _, chans = proj.shape
    depth, outs = out_weight.shape
    taps, reach = short_filter.shape[0], medium_filter.shape[0]
    length, chunks = rows + reach, chans // WIDE
    tables = jnp.asarray(spectrum_tables(length, reach))
    dma = pltpu.SemaphoreType.DMA
    return pl.pallas_call(
        functools.partial(kernel, n_ctx, n_tp, taps),
        out_shape=jax.ShapeDtypeStruct((rows, outs), jnp.bfloat16),
        in_specs=[pl.BlockSpec(memory_space=pltpu.HBM)] * 7,
        out_specs=pl.BlockSpec(memory_space=pltpu.VMEM),
        scratch_shapes=[
            pltpu.VMEM(residual.shape, residual.dtype),
            pltpu.VMEM((3, rows, chans), proj.dtype),
            pltpu.VMEM((3, taps, chans), short_filter.dtype),
            pltpu.VMEM(medium_filter.shape, medium_filter.dtype),
            pltpu.VMEM((1, chans), skip.dtype),
            pltpu.VMEM(tables.shape, jnp.float32),
            pltpu.VMEM(tables.shape, jnp.bfloat16),
            pltpu.VMEM((n_ctx * depth, outs), jnp.bfloat16),
            pltpu.VMEM((n_tp, chunks, rows, WIDE), jnp.bfloat16),
            pltpu.VMEM((rows, outs), jnp.float32),
            pltpu.VMEM((3, EDGE + rows, chans), jnp.float32),
            pltpu.VMEM((3, 8, chans), jnp.float32),
            pltpu.VMEM((length, chans), jnp.bfloat16),
            pltpu.VMEM((length, chans), jnp.float32),
            pltpu.VMEM((rows, chans), jnp.float32),
            pltpu.VMEM((length, WIDE), jnp.float32),
            pltpu.VMEM((length, WIDE), jnp.bfloat16),
            pltpu.VMEM((3, EDGE, chans), jnp.bfloat16),
            dma((8,)),
            dma,
            dma((max(n_ctx, 7 * PIECES),)),
            dma((max(n_ctx, 7 * PIECES),)),
            dma((2, n_tp - 1, 2, chunks)),
            dma((2, n_tp - 1, 2, chunks)),
            dma,
            dma,
            dma((chunks,)),
            dma((chunks,)),
        ],
        compiler_params=pltpu.CompilerParams(
            collective_id=0, has_side_effects=True, vmem_limit_bytes=44 * 2**20
        ),
        cost_estimate=pl.CostEstimate(
            flops=2 * rows * n_ctx * depth * outs, bytes_accessed=2 * rows * chans * 5, transcendentals=0
        ),
    )(*(
        pltpu.with_memory_space_constraint(array, pltpu.HBM)
        for array in (
            residual, proj.transpose(1, 0, 2), short_filter.transpose(1, 0, 2), medium_filter,
            skip.reshape(1, chans), out_weight, tables,
        )
    ))


def solution(mesh):
    in_specs = (
        P("ctx", "tp"),
        P("ctx", None, "tp"),
        P(None, None, "tp"),
        P(None, "tp"),
        P("tp"),
        P("ctx", "tp"),
    )
    return jax.shard_map(
        functools.partial(on_device, mesh.shape["ctx"], mesh.shape["tp"]),
        mesh=mesh, in_specs=in_specs, out_specs=P("ctx", "tp"), check_vma=False,
    )
```

```python
import functools

import jax
import jax.numpy as jnp
import numpy as np
from jax import lax
from jax.experimental import pallas as pl
from jax.experimental.pallas import tpu as pltpu
from jax.sharding import PartitionSpec as P

WIDE = 256
STEP = 64
PIECES = 8
WINDOW = 6
EDGE = 16
MESH = pl.DeviceIdType.MESH


def spectrum_tables(length, reach):
    half = length // 2
    angle = 2 * np.pi / length * np.outer(np.arange(half) + 0.5, np.arange(length))
    forward = np.concatenate([np.cos(angle), np.sin(angle)], 0)
    inverse = (2.0 / length) * forward.T[reach:]

    return np.concatenate([forward, inverse], 0).astype(np.float32)


def dot(a, b):
    return jnp.dot(a, b, preferred_element_type=jnp.float32)


def kernel(
    n_ctx, n_tp, taps,
    residual_hbm, proj_hbm, short_hbm, medium_hbm, skip_hbm, weight,
    tables_hbm,
    out,
    residual, proj, short, medium, skip, tables32, tables,
    whole, gated, total, wide, short32, product, transfer, query, spec, spec_out, edge,
    local_sem, own_sem, w_send, w_recv, z_send, z_recv, edge_send, edge_recv, tail_send, tail_recv,
):
    rows, chans = residual.shape[0], proj.shape[2]
    depth, outs = weight.shape
    reach = medium.shape[0]
    chunks = chans // WIDE
    length = rows + reach
    half = length // 2
    me, z = lax.axis_index("ctx"), lax.axis_index("tp")
    after, before = lax.rem(me + 1, n_ctx), lax.rem(me + n_ctx - 1, n_ctx)
    square = n_ctx == 8 and n_tp == 4 and chans == 2 * depth

    def flip(bit):
        return me + bit - 2 * bit * lax.rem(me // bit, 2)

    if square:
        core, side, up = flip(1), flip(2), flip(4)
        corner = side + up - me

    barrier = pltpu.get_barrier_semaphore()

    def greet(where):
        pl.semaphore_signal(barrier, inc=1, device_id=where, device_id_type=MESH)

    if square:
        for peer in (core, side, up, after, before):
            greet({"ctx": peer})
        greeted = 5
    else:
        @pl.loop(1, n_ctx)
        def _(by):
            greet({"ctx": lax.rem(me + by, n_ctx)})
        greeted = n_ctx - 1

    @pl.when(z < n_tp - 1)
    def _():
        greet({"tp": z + 1})

    @pl.when(z > 0)
    def _():
        greet({"tp": z - 1})

    first = rows - reach

    def bring(n, source, target):
        copy = pltpu.make_async_copy(source, target, local_sem.at[n])
        copy.start()
        return copy

    later = pl.ds(first, reach)
    get_short = bring(0, short_hbm, short)
    get_tail = bring(1, proj_hbm.at[1:3, later, :], proj.at[1:3, later, :])
    get_head = bring(2, proj_hbm.at[1:3, 0:first, :], proj.at[1:3, 0:first, :])
    get_query = bring(3, proj_hbm.at[0], proj.at[0])
    get_medium = bring(4, medium_hbm, medium)
    get_tables = bring(5, tables_hbm, tables32)
    get_rest = [bring(6, skip_hbm, skip), bring(7, residual_hbm, residual)]
    forward, inverse = tables.at[0:length, :], tables.at[pl.ds(length, rows), :]

    def columns(q):
        return pl.ds(pl.multiple_of(q * WIDE, WIDE), WIDE)

    def edge_copy():
        return pltpu.make_async_remote_copy(
            src_ref=proj_hbm.at[:, pl.ds(rows - EDGE, EDGE), :], dst_ref=edge,
            send_sem=edge_send, recv_sem=edge_recv, device_id={"ctx": after}, device_id_type=MESH)

    def tail_copy(q):
        return pltpu.make_async_remote_copy(
            src_ref=product.at[pl.ds(rows, reach), columns(q)],
            dst_ref=product.at[pl.ds(0, reach), columns(q)],
            send_sem=tail_send.at[q], recv_sem=tail_recv.at[q],
            device_id={"ctx": after}, device_id_type=MESH)

    cut = reach + EDGE
    spans = [(cut, rows - cut), (0, cut)]

    def z_copy(way, step, piece, origin):
        part_of, q = piece
        there = gated.at[origin, q, pl.ds(*spans[part_of]), :]
        return pltpu.make_async_remote_copy(
            src_ref=there, dst_ref=there,
            send_sem=z_send.at[way, step, part_of, q], recv_sem=z_recv.at[way, step, part_of, q],
            device_id={"tp": z + 1 if way == 0 else z - 1}, device_id_type=MESH)

    def z_sends(step, q, act):
        @pl.when((z < n_tp - 1) & (z >= step))
        def _():
            act(z_copy(0, step, q, z - step))

        @pl.when((z > 0) & (z + step <= n_tp - 1))
        def _():
            act(z_copy(1, step, q, z + step))

    def z_wait(step, q):
        @pl.when(z - 1 - step >= 0)
        def _():
            z_copy(0, step, q, z - 1 - step).wait_recv()

        @pl.when(z + 1 + step <= n_tp - 1)
        def _():
            z_copy(1, step, q, z + 1 + step).wait_recv()

    def z_pass(step, q):
        z_wait(step, q)
        if step + 1 < n_tp - 1:
            z_sends(step + 1, q, lambda copy: copy.start())

    part = depth // PIECES
    to_side = [*range(PIECES)]
    to_up = to_side[PIECES // 2 :] + to_side[: PIECES // 2]
    ticks = PIECES + PIECES // 2

    def w_copy(slot, block, piece, to, own=False):
        rows_there = pl.ds(pl.multiple_of(block * depth + piece * part, part), part)
        return pltpu.make_async_remote_copy(
            src_ref=weight.at[pl.ds(piece * part, part), :] if own else whole.at[rows_there, :],
            dst_ref=whole.at[rows_there, :],
            send_sem=w_send.at[slot], recv_sem=w_recv.at[slot],
            device_id={"ctx": to}, device_id_type=MESH)

    sent = []

    def launch(copy):
        copy.start()
        sent.append(copy)

    def w_tick(t):
        if t < PIECES:
            launch(w_copy(t, me, to_side[t], side, own=True))
            launch(w_copy(ticks + t, me, to_up[t], up, own=True))
        else:
            launch(w_copy(t, up, to_up[t - PIECES], side))
            launch(w_copy(ticks + t, side, to_side[t - PIECES], up))

    def w_come(t):
        if t < PIECES:
            return (t, side, to_side[t]), (ticks + t, up, to_up[t])
        return (t, corner, to_up[t - PIECES]), (ticks + t, corner, to_side[t - PIECES])

    def w_take(t):
        for slot, block, piece in w_come(t):
            w_copy(slot, block, piece, side if slot < ticks else up).wait_recv()
            launch(w_copy(2 * ticks + slot, block, piece, core))

    def w_core(t):
        for slot, block, piece in w_come(t):
            w_copy(2 * ticks + slot, block + core - me, piece, core).wait_recv()

    def w_all(by):
        return pltpu.make_async_remote_copy(
            src_ref=weight, dst_ref=whole.at[pl.ds(pl.multiple_of(me * depth, depth), depth), :],
            send_sem=w_send.at[by], recv_sem=w_recv.at[by],
            device_id={"ctx": lax.rem(me + by, n_ctx)}, device_id_type=MESH)

    own = pltpu.make_async_copy(
        weight, whole.at[pl.ds(pl.multiple_of(me * depth, depth), depth), :], own_sem)

    def mixed(stream, start, count, cols):
        acc = None
        for j in range(taps):
            term = short32[stream, j : j + 1, cols] * wide[stream, pl.ds(EDGE + start - j, count), cols]
            acc = term if acc is None else acc + term
        return acc

    def multiply(start, count, cols):
        product[pl.ds(reach + start, count), cols] = (
            mixed(1, start, count, cols) * mixed(2, start, count, cols)
        ).astype(jnp.bfloat16)

    def widen(stream, start, count, cols):
        wide[stream, pl.ds(EDGE + start, count), cols] = proj[stream, pl.ds(start, count), cols].astype(jnp.float32)

    def before_edge(q):
        cols = columns(q)
        for stream in (1, 2):
            widen(stream, 0, first, cols)
        widen(0, 0, rows, cols)
        spots = [(EDGE, STEP - EDGE)] + [(start, STEP) for start in range(STEP, rows, STEP)]
        for start, count in spots:
            if start < first:
                multiply(start, count, cols)
            query[pl.ds(start, count), cols] = mixed(0, start, count, cols)

    get_short.wait()
    for stream in range(3):
        short32[stream, 0:taps, :] = short[stream].astype(jnp.float32)
    get_tail.wait()
    get_head.wait()

    @pl.loop(0, chunks)
    def _(q):
        cols = columns(q)
        for stream in (1, 2):
            widen(stream, first - EDGE, reach + EDGE, cols)
        for start in range(first, rows, STEP):
            multiply(start, STEP, cols)

    get_tables.wait()

    @pl.loop(0, (length + rows) // 64)
    def _(at):
        span = pl.ds(pl.multiple_of(at * 64, 64), 64)
        tables[span, :] = tables32[span, :].astype(jnp.bfloat16)

    pl.semaphore_wait(barrier, greeted + jnp.where(z < n_tp - 1, 1, 0) + jnp.where(z > 0, 1, 0))
    edge_copy().start()
    for q in range(chunks):
        tail_copy(q).start()
    if square:
        for t in range(WINDOW):
            w_tick(t)
        for piece in range(PIECES):
            launch(w_copy(4 * ticks + piece, me, piece, core, own=True))
    else:
        @pl.loop(1, n_ctx)
        def _(by):
            w_all(by).start()
    own.start()

    get_query.wait()
    before_edge(0)

    get_medium.wait()

    @pl.loop(0, chunks)
    def _(q):
        taps_now = medium[:, columns(q)]
        transfer[:, columns(q)] = dot(forward[:, 0:reach], taps_now)

    for copy in get_rest:
        copy.wait()
    def gate(part_of, q, skipped):
        cols = columns(q)
        start, count = spans[part_of]
        window = product[skipped:, cols]
        spec[...] = dot(forward[:, skipped:], window)
        for top in range(0, half, 64):
            a, b = spec[top : top + 64, :], spec[half + top : half + top + 64, :]
            c, d = transfer[top : top + 64, cols], transfer[half + top : half + top + 64, cols]
            for at, value in ((top, a * c - b * d), (half + top, a * d + b * c)):
                spec_out[at : at + 64, :] = value.astype(jnp.bfloat16)
        filtered = dot(inverse[pl.ds(start, count), :], spec_out[...])
        filtered = filtered + skip[:, cols] * product[pl.ds(reach + start, count), cols].astype(jnp.float32)
        gated[z, q, pl.ds(start, count), :] = (query[pl.ds(start, count), cols] * filtered).astype(jnp.bfloat16)
        z_sends(0, (part_of, q), lambda copy: copy.start())

    @pl.loop(0, chunks)
    def _(q):
        product[pl.ds(reach, EDGE), columns(q)] = jnp.zeros((EDGE, WIDE), jnp.bfloat16)
        gate(0, q, reach)

        @pl.when(q + 1 < chunks)
        def _():
            before_edge(q + 1)

    edge_copy().wait_recv()
    for stream in range(3):
        wide[stream, 0:EDGE, :] = jnp.where(me > 0, edge[stream].astype(jnp.float32), 0.0)

    @pl.loop(0, chunks)
    def _(q):
        cols = columns(q)
        multiply(0, EDGE, cols)
        query[0:EDGE, cols] = mixed(0, 0, EDGE, cols)
        tail_copy(q).wait_recv()

        @pl.when(me == 0)
        def _():
            product[0:reach, cols] = jnp.zeros((reach, WIDE), jnp.bfloat16)

        gate(1, q, 0)

    def project(origin, begin, count):
        @pl.loop(0, outs // WIDE)
        def _(tile):
            cols = columns(tile)
            acc = total[:, cols]
            for q in range(begin, begin + count):
                at = pl.multiple_of(origin * chans + q * WIDE, WIDE)
                acc = acc + dot(gated[origin, q], whole[pl.ds(at, WIDE), cols])
            total[:, cols] = acc

    total[...] = residual[...].astype(jnp.float32)
    def near(origin):
        return (origin - z <= n_tp - 2) & (z - origin <= n_tp - 2)

    def last_z():
        for part_of in range(2):
            for q in range(chunks):
                z_wait(n_tp - 2, (part_of, q))

    if square:
        far = corner // 2
        events = [(step, (part_of, q)) for step in range(n_tp - 2) for part_of in range(2) for q in range(chunks)]
        for t in range(ticks):
            for event in events[2 * t : 2 * t + 2]:
                z_pass(*event)
            w_take(t)
            if t + WINDOW < ticks:
                w_tick(t + WINDOW)
            if t == PIECES:
                own.wait()
                for piece in range(PIECES):
                    w_copy(4 * ticks + piece, core, piece, core).wait_recv()
                for early in range(PIECES):
                    w_core(early)

                @pl.loop(0, n_tp)
                def _(origin):
                    @pl.when(near(origin) & (origin != far))
                    def _():
                        project(origin, 0, chunks)

        last_z()

        @pl.when(((z == 0) | (z == n_tp - 1)) & (n_tp - 1 - z != far))
        def _():
            project(n_tp - 1 - z, 0, chunks)

        for late in range(PIECES, ticks):
            w_core(late)
        project(far, 0, chunks)
    else:
        for step in range(n_tp - 2):
            @pl.loop(0, chunks)
            def _(q):
                z_pass(step, (0, q))

            @pl.loop(0, chunks)
            def _(q):
                z_pass(step, (1, q))

        own.wait()

        @pl.loop(1, n_ctx)
        def _(by):
            w_all(by).wait_recv()

        @pl.loop(0, n_tp)
        def _(origin):
            @pl.when(near(origin))
            def _():
                project(origin, 0, chunks)

        last_z()

        @pl.when((z == 0) | (z == n_tp - 1))
        def _():
            project(n_tp - 1 - z, 0, chunks)

    out[...] = total[...].astype(jnp.bfloat16)

    edge_copy().wait_send()
    for q in range(chunks):
        tail_copy(q).wait_send()
    if square:
        for copy in sent:
            copy.wait_send()
    else:
        @pl.loop(1, n_ctx)
        def _(by):
            w_all(by).wait_send()
    for step in range(n_tp - 1):
        @pl.loop(0, chunks)
        def _(q):
            for part_of in range(2):
                z_sends(step, (part_of, q), lambda copy: copy.wait_send())


def on_device(n_ctx, n_tp, residual, proj, short_filter, medium_filter, skip, out_weight):
    rows, _, chans = proj.shape
    depth, outs = out_weight.shape
    taps, reach = short_filter.shape[0], medium_filter.shape[0]
    length, chunks = rows + reach, chans // WIDE
    tables = jnp.asarray(spectrum_tables(length, reach))
    dma = pltpu.SemaphoreType.DMA
    return pl.pallas_call(
        functools.partial(kernel, n_ctx, n_tp, taps),
        out_shape=jax.ShapeDtypeStruct((rows, outs), jnp.bfloat16),
        in_specs=[pl.BlockSpec(memory_space=pltpu.HBM)] * 7,
        out_specs=pl.BlockSpec(memory_space=pltpu.VMEM),
        scratch_shapes=[
            pltpu.VMEM(residual.shape, residual.dtype),
            pltpu.VMEM((3, rows, chans), proj.dtype),
            pltpu.VMEM((3, taps, chans), short_filter.dtype),
            pltpu.VMEM(medium_filter.shape, medium_filter.dtype),
            pltpu.VMEM((1, chans), skip.dtype),
            pltpu.VMEM(tables.shape, jnp.float32),
            pltpu.VMEM(tables.shape, jnp.bfloat16),
            pltpu.VMEM((n_ctx * depth, outs), jnp.bfloat16),
            pltpu.VMEM((n_tp, chunks, rows, WIDE), jnp.bfloat16),
            pltpu.VMEM((rows, outs), jnp.float32),
            pltpu.VMEM((3, EDGE + rows, chans), jnp.float32),
            pltpu.VMEM((3, 8, chans), jnp.float32),
            pltpu.VMEM((length, chans), jnp.bfloat16),
            pltpu.VMEM((length, chans), jnp.float32),
            pltpu.VMEM((rows, chans), jnp.float32),
            pltpu.VMEM((length, WIDE), jnp.float32),
            pltpu.VMEM((length, WIDE), jnp.bfloat16),
            pltpu.VMEM((3, EDGE, chans), jnp.bfloat16),
            dma((8,)),
            dma,
            dma((max(n_ctx, 7 * PIECES),)),
            dma((max(n_ctx, 7 * PIECES),)),
            dma((2, n_tp - 1, 2, chunks)),
            dma((2, n_tp - 1, 2, chunks)),
            dma,
            dma,
            dma((chunks,)),
            dma((chunks,)),
        ],
        compiler_params=pltpu.CompilerParams(
            collective_id=0, has_side_effects=True, vmem_limit_bytes=44 * 2**20
        ),
        cost_estimate=pl.CostEstimate(
            flops=2 * rows * n_ctx * depth * outs, bytes_accessed=2 * rows * chans * 5, transcendentals=0
        ),
    )(*(
        pltpu.with_memory_space_constraint(array, pltpu.HBM)
        for array in (
            residual, proj.transpose(1, 0, 2), short_filter.transpose(1, 0, 2), medium_filter,
            skip.reshape(1, chans), out_weight, tables,
        )
    ))


def solution(mesh):
    in_specs = (
        P("ctx", "tp"),
        P("ctx", None, "tp"),
        P(None, None, "tp"),
        P(None, "tp"),
        P("tp"),
        P("ctx", "tp"),
    )
    return jax.shard_map(
        functools.partial(on_device, mesh.shape["ctx"], mesh.shape["tp"]),
        mesh=mesh, in_specs=in_specs, out_specs=P("ctx", "tp"), check_vma=False,
    )
```
